256 devices in a mesh: energy: 32 (over z, y_lo, core), cell: 8 (over x, y_hi).
Axes of the slice: x: 4, y: 4 (y_hi: 2, y_lo: 2; y = y_hi * 2 + y_lo), z: 8, core: 2. Of those that a mesh axis runs over, the one named last changes fastest.
Arguments:
- glesser: float32 [16, 128, 2, 9216], P('cell', 'energy'), may hold values from -4 to 4, as said below
- wlesser: float32 [16, 128, 2, 9216], P('cell', 'energy'), may hold values from -4 to 4, as said below
- gret_diag: float32 [16, 128, 2, 9216], P('cell', 'energy'), may hold values from -0.4375 to 0.4375
- gret_upper: float32 [16, 128, 2, 9216], P('cell', 'energy'), may hold values from -0.4375 to 0.4375
Outputs:
- sigma_lesser: float32 [16, 128, 2, 9216], P('cell', 'energy')
- g_lesser_new: float32 [16, 128, 2, 9216], P('cell', 'energy')
The draws below stay inside these ranges and needn't reach their ends.
Inputs may be any that keep to these rules, and one draw needn't show every extreme that they name: Each block of glesser is anti-Hermitian: its real part is antisymmetric and its imaginary part symmetric. Each block of wlesser is anti-Hermitian: its real part is antisymmetric and its imaginary part symmetric.
All inputs are finite; a program needn't handle non-finite values.
Results may differ from the reference program's by a relative error of at most 0.000098.
Values sent between devices are 32-bit elements; how exact they have to be, the bound alone decides.
A program may use at most 128 MiB of HBM per device.

```python
import jax
import jax.numpy as jnp
from jax import lax

B = 96
CELLS = 16
NE = 128


def anti_hermitian(key):
    real_key, imag_key = jax.random.split(key, 2)
    shape_all = (CELLS, NE, B, B)
    real_part = jnp.clip(jax.random.normal(real_key, shape_all, jnp.float32), -4.0, 4.0)
    imag_part = jnp.clip(jax.random.normal(imag_key, shape_all, jnp.float32), -4.0, 4.0)
    real_part = 0.5 * (real_part - jnp.swapaxes(real_part, -1, -2))
    imag_part = 0.5 * (imag_part + jnp.swapaxes(imag_part, -1, -2))
    return jnp.stack([real_part, imag_part], 2).reshape(CELLS, NE, 2, B * B)


def draw_glesser(key, part):
    return anti_hermitian(jax.random.fold_in(key, 11))


def draw_wlesser(key, part):
    return anti_hermitian(jax.random.fold_in(key, 23))


def block_scale(stream_key, extent, pieces, low, largest):
    level = 1.0
    for position, shards_of in pieces:
        draws = jax.random.uniform(jax.random.fold_in(jax.random.fold_in(stream_key, 6), position), (shards_of,), jnp.float32, low / len(pieces), largest / len(pieces))
        level = level * jnp.repeat(jnp.exp(draws), extent[position] // shards_of).reshape((-1,) + (1,) * (len(extent) - 1 - position))
    return level


def normal_values(own_key, dims, spread, most, shards=(), held_as=jnp.bfloat16):
    drawn = spread * jax.random.normal(own_key, dims, jnp.float32)
    if shards:
        drawn = drawn * block_scale(own_key, dims, shards, -0.22, 0.18)
    return jnp.clip(drawn, -most, most).astype(held_as)


def setup_inputs(seed: int = 0) -> dict:
    key_list = jax.random.split(jax.random.key(seed), 5)
    glesser = draw_glesser(jax.random.fold_in(key_list[4], 71), 0)
    wlesser = draw_wlesser(jax.random.fold_in(key_list[4], 71), 0)
    gret_diag = normal_values(key_list[2], (CELLS, NE, 2, B * B), (2 * B) ** -0.5, 0.4375, ((0, 8), (1, 32)), jnp.float32)
    gret_upper = normal_values(key_list[3], (CELLS, NE, 2, B * B), (2 * B) ** -0.5, 0.4375, ((0, 8), (1, 32)), jnp.float32)
    return dict(glesser=glesser, wlesser=wlesser, gret_diag=gret_diag, gret_upper=gret_upper)


HIGHEST = lax.Precision.HIGHEST


def to_pairs(flat):
    blocks = flat.reshape(flat.shape[:-2] + (2, B, B))
    return jnp.concatenate([blocks[..., 0, :, :], blocks[..., 1, :, :]], -1)


def from_pairs(pair_block):
    real_part = pair_block[..., :B]
    imag_part = pair_block[..., B:]
    return jnp.stack([real_part, imag_part], -3).reshape(pair_block.shape[:-2] + (2, B * B))


def block_matrix(right_block):
    width = right_block.shape[-1] // 2
    real_part = right_block[..., :width]
    imag_part = right_block[..., width:]
    top_rows = jnp.concatenate([real_part, imag_part], -1)
    bottom_rows = jnp.concatenate([-imag_part, real_part], -1)
    return jnp.concatenate([top_rows, bottom_rows], -2)


def complex_product(left_block, right_block):
    return jnp.einsum("...ij,...jk->...ik", left_block, block_matrix(right_block), precision=HIGHEST)


def conjugate_transpose(block_pair):
    width = block_pair.shape[-1] // 2
    real_part = jnp.swapaxes(block_pair[..., :width], -1, -2)
    imag_part = jnp.swapaxes(block_pair[..., width:], -1, -2)
    return jnp.concatenate([real_part, -imag_part], -1)


def plain_transpose(block_pair):
    width = block_pair.shape[-1] // 2
    real_part = jnp.swapaxes(block_pair[..., :width], -1, -2)
    imag_part = jnp.swapaxes(block_pair[..., width:], -1, -2)
    return jnp.concatenate([real_part, imag_part], -1)


def sandwich(outer_block, middle):
    return complex_product(complex_product(outer_block, middle), conjugate_transpose(outer_block))


def convolve_cell(operands):
    green_cell, screen_cell = operands
    steps_count = green_cell.shape[0]
    green_complex = lax.complex(green_cell[:, 0], green_cell[:, 1])
    screen_complex = lax.complex(screen_cell[:, 0], screen_cell[:, 1])
    spectrum = jnp.fft.fft(green_complex, n=2 * steps_count, axis=0) * jnp.fft.fft(screen_complex, n=2 * steps_count, axis=0)
    result = jnp.fft.ifft(spectrum, axis=0)[:steps_count]
    factor = steps_count ** -0.5
    return jnp.stack([-jnp.imag(result) * factor, jnp.real(result) * factor], 1).astype(jnp.float32)


def reference(glesser, wlesser, gret_diag, gret_upper):
    self_flat = lax.map(convolve_cell, (glesser, wlesser))
    self_energy = to_pairs(self_flat)
    diag_pairs = to_pairs(gret_diag)
    upper_pairs = to_pairs(gret_upper)
    zero_cell = jnp.zeros_like(self_energy[:1])
    energy_below = jnp.concatenate([zero_cell, self_energy[:-1]], 0)
    energy_above = jnp.concatenate([self_energy[1:], zero_cell], 0)
    lower_source = jnp.concatenate([jnp.zeros_like(upper_pairs[:1]), upper_pairs[:-1]], 0)

    def one_cell(operands):
        diag_block, upper_block, lower_block, own_energy, below_energy, above_energy = operands
        center = sandwich(diag_block, own_energy)
        from_below = sandwich(plain_transpose(lower_block), below_energy)
        from_above = sandwich(upper_block, above_energy)
        return center + from_below + from_above

    lesser_new = lax.map(one_cell, (diag_pairs, upper_pairs, lower_source, self_energy, energy_below, energy_above))
    return self_flat, from_pairs(lesser_new)
```

```python
import functools

import jax
import jax.numpy as jnp
import ml_dtypes
import numpy as np
from jax import lax
from jax.experimental import pallas as pl
from jax.experimental.pallas import tpu as pltpu
from jax.sharding import PartitionSpec as P

MESH = pl.DeviceIdType.MESH
B = 96
NE = 128
PEERS = 32
HALF = 36
F32 = jnp.float32
BF16 = jnp.bfloat16
VMEM_LIMIT = 56 * 1024 * 1024


def two_terms(x):
    high = x.astype(ml_dtypes.bfloat16)
    return high, (x - high.astype(np.float64)).astype(ml_dtypes.bfloat16)


def transforms():
    n = np.arange(NE)
    k = np.arange(NE)
    angle = 2.0 * np.pi / (4 * NE) * ((n[None, :] * (1 - 4 * k[:, None])) % (4 * NE))
    forward = np.zeros((2, 2, NE, NE, 2))
    inverse = np.zeros((NE, 2, 2, 2, NE))
    scale = NE ** -0.5 / NE
    for part in range(2):
        forward[part, 0, :, :, part] = np.cos(angle)
        forward[part, 1, :, :, part] = np.sin(angle)
        inverse[:, part, part, 0, :] = np.cos(angle).T * scale
        inverse[:, part, part, 1, :] = np.sin(angle).T * scale
    return forward.reshape(512, 256), inverse.reshape(256, 512)


def split(x):
    high = x.astype(BF16)
    return high, (x - high.astype(F32)).astype(BF16)


def dot3(ah, al, bh, bl, dims=(((1,), (0,)), ((), ()))):
    d = functools.partial(lax.dot_general, dimension_numbers=dims, preferred_element_type=F32)
    return d(ah, bh) + (d(al, bh) + d(ah, bl))


def whole(ref, sem):
    return pltpu.make_async_copy(ref, ref, sem)


def exchange_kernel(
    g_hbm, w_hbm, u_hbm, fh, fl, ih, il,
    sg, above, below, ub,
    gv, wv, pk, rv, ob,
    load_sem, self_sem, send_sem, xsend_sem, recv_sem, back_sem, xback_sem, sig_sem, hop_send, hop_recv,
):
    me = lax.axis_index("energy")
    k = lax.axis_index("cell")
    my_z = me // 4
    my_i = my_z // 2
    my_c = my_z % 2
    is_extra = jnp.equal(me % 4, my_i)
    has_up = k < 7
    has_down = k > 0

    for c in range(2):
        pltpu.make_async_copy(g_hbm.at[pl.ds(4 * c, 4)], gv.at[pl.ds(4 * c, 4), pl.ds(0, 144)], load_sem.at[c, 0]).start()
        pltpu.make_async_copy(w_hbm.at[pl.ds(4 * c, 4)], wv.at[pl.ds(4 * c, 4), pl.ds(0, 144)], load_sem.at[c, 1]).start()

    barrier = pltpu.get_barrier_semaphore()

    def greet(i, carry):
        pl.semaphore_signal(barrier, inc=1, device_id={"energy": lax.rem(me + i, PEERS)}, device_id_type=MESH)
        return carry

    lax.fori_loop(1, PEERS, greet, 0)

    @pl.when(has_up)
    def _():
        pl.semaphore_signal(barrier, inc=1, device_id={"cell": k + 1}, device_id_type=MESH)

    @pl.when(has_down)
    def _():
        pl.semaphore_signal(barrier, inc=1, device_id={"cell": k - 1}, device_id_type=MESH)

    row = lax.broadcasted_iota(jnp.int32, (40, 128), 0)
    lane = lax.broadcasted_iota(jnp.int32, (40, 128), 1)
    slot_index = row * 128 + lane
    a_index = (slot_index * 43691) >> 22
    b_index = slot_index - a_index * B
    direct = b_index >= a_index
    diagonal = b_index == a_index
    near = lane >= 48

    def pack(c):
        for which, source in enumerate((gv, wv)):
            pltpu.make_async_copy(
                (g_hbm, w_hbm)[which].at[pl.ds(4 * c, 4)], source.at[pl.ds(4 * c, 4), pl.ds(0, 144)], load_sem.at[c, which]
            ).wait()

            def one(e, carry):
                blk = 4 * c + e
                first, far = [], []
                for part in range(2):
                    first.append(source[blk, pl.ds(part, 40, stride=2), :])
                    here = source[blk, pl.ds(72 + part, 40, stride=2), :]
                    after = source[blk, pl.ds(74 + part, 40, stride=2), :]
                    far.append(pltpu.roll(jnp.where(near, here, after), 80, 1))
                re = jnp.where(direct, first[0], far[0])
                re = jnp.where(diagonal, far[1], re)
                im = jnp.where(direct, first[1], far[1])
                base = which * 8 + 2 * e
                pk[c, pl.ds(base, 40, stride=16), :] = re
                pk[c, pl.ds(base + 1, 40, stride=16), :] = im
                return carry

            lax.fori_loop(0, 4, one, 0)

    def outgoing(c, p):
        return pltpu.make_async_remote_copy(
            src_ref=pk.at[c, pl.ds(p * 16, 16)], dst_ref=rv.at[c, me], send_sem=send_sem.at[c], recv_sem=recv_sem.at[c],
            device_id={"energy": p}, device_id_type=MESH,
        )

    def extra_out(c, i):
        return pltpu.make_async_remote_copy(
            src_ref=pk.at[c, pl.ds((PEERS + i) * 16, 16)], dst_ref=rv.at[2, me], send_sem=xsend_sem.at[c, i],
            recv_sem=recv_sem.at[2], device_id={"energy": 4 * (2 * i + c) + i}, device_id_type=MESH,
        )

    def send(c):
        def start(i, carry):
            outgoing(c, lax.rem(me + i, PEERS)).start()
            return carry

        pltpu.make_async_copy(pk.at[c, pl.ds(me * 16, 16)], rv.at[c, me], recv_sem.at[c]).start()
        lax.fori_loop(1, PEERS, start, 0)
        for i in range(4):
            mine = jnp.equal(me, 4 * (2 * i + c) + i)

            @pl.when(jnp.logical_not(mine))
            def _(i=i):
                extra_out(c, i).start()

            @pl.when(mine)
            def _(i=i):
                pltpu.make_async_copy(pk.at[c, pl.ds((PEERS + i) * 16, 16)], rv.at[2, me], recv_sem.at[2]).start()

    pack(0)
    pl.semaphore_wait(barrier, 31 + has_up.astype(jnp.int32) + has_down.astype(jnp.int32))
    send(0)
    pack(1)
    send(1)

    def u_copy():
        return pltpu.make_async_remote_copy(
            src_ref=u_hbm.at[pl.ds(4, 4)], dst_ref=ub, send_sem=hop_send.at[0], recv_sem=hop_recv.at[0],
            device_id={"cell": k + 1}, device_id_type=MESH,
        )

    def down_copy():
        return pltpu.make_async_remote_copy(
            src_ref=sg.at[0], dst_ref=above, send_sem=hop_send.at[1], recv_sem=hop_recv.at[1],
            device_id={"cell": k - 1}, device_id_type=MESH,
        )

    def up_copy():
        return pltpu.make_async_remote_copy(
            src_ref=sg.at[1], dst_ref=below, send_sem=hop_send.at[2], recv_sem=hop_recv.at[2],
            device_id={"cell": k + 1}, device_id_type=MESH,
        )

    @pl.when(has_up)
    def _():
        u_copy().start()

    @pl.when(jnp.logical_not(has_up))
    def _():
        above[...] = jnp.zeros_like(above)

    @pl.when(jnp.logical_not(has_down))
    def _():
        below[...] = jnp.zeros_like(below)
        ub[...] = jnp.zeros_like(ub)

    def back(slot, c, tile, p):
        return pltpu.make_async_remote_copy(
            src_ref=ob.at[slot, p], dst_ref=sg.at[c, tile], send_sem=back_sem.at[slot], recv_sem=sig_sem.at[c],
            device_id={"energy": p}, device_id_type=MESH,
        )

    def convolve(slot, c, tile):
        whole(rv.at[slot], recv_sem.at[slot]).wait()
        green = rv[slot, :, 0:8, :].reshape(256, 128)
        screen = rv[slot, :, 8:16, :].reshape(256, 128)
        xh, xl = split(jnp.concatenate([green, screen], 1))
        hat = dot3(fh[...], fl[...], xh, xl)
        xr, xi, yr, yi = (hat[128 * j:128 * j + 128] for j in range(4))
        xrg, xrw, xig, xiw = xr[:, :128], xr[:, 128:], xi[:, :128], xi[:, 128:]
        yrg, yrw, yig, yiw = yr[:, :128], yr[:, 128:], yi[:, :128], yi[:, 128:]
        xx_r = xrg * xrw - xig * xiw
        xx_i = xrg * xiw + xig * xrw
        yy_r = yrg * yrw - yig * yiw
        yy_i = yrg * yiw + yig * yrw
        xy_r = (xrg * yrw - xig * yiw) + (yrg * xrw - yig * xiw)
        xy_i = (xrg * yiw + xig * yrw) + (yrg * xiw + yig * xrw)
        main = jnp.concatenate([-xy_r, -xy_i, xx_r - yy_r, xx_i - yy_i], 0)
        diag = jnp.concatenate([-xx_r, -xx_i, -yy_r, -yy_i], 0)
        zh, zl = split(jnp.concatenate([main, diag], 1))
        out = dot3(ih[...], il[...], zh, zl)
        position = tile * 128 + lax.broadcasted_iota(jnp.int32, (256, 128), 1)
        on_diagonal = position == ((position * 43241) >> 22) * 97
        ob[slot] = jnp.where(on_diagonal, out[:, 128:], out[:, :128]).reshape(PEERS, 8, 128)

        pltpu.make_async_copy(ob.at[slot, me], sg.at[c, tile], sig_sem.at[c]).start()

        def start(i, carry):
            back(slot, c, tile, lax.rem(me + i, PEERS)).start()
            return carry

        lax.fori_loop(1, PEERS, start, 0)

    def phase(c, carry):
        def step(j, inner):
            slot = jnp.where(j == 0, c, 2)
            tile = jnp.where(j == 0, me, PEERS + my_i)
            convolve(slot, c, tile)
            return inner

        count = 1 + jnp.where(jnp.logical_and(is_extra, my_c == c), 1, 0)
        lax.fori_loop(0, count, step, 0)
        return carry

    lax.fori_loop(0, 2, phase, 0)

    whole(sg.at[0], sig_sem.at[0]).wait()

    @pl.when(has_down)
    def _():
        down_copy().start()

    whole(sg.at[1], sig_sem.at[1]).wait()

    @pl.when(has_up)
    def _():
        up_copy().start()

    for c in range(2):
        whole(pk.at[c, pl.ds(0, 31 * 16)], send_sem.at[c]).wait()
        for i in range(4):
            @pl.when(jnp.logical_not(jnp.equal(me, 4 * (2 * i + c) + i)))
            def _(c=c, i=i):
                extra_out(c, i).wait_send()
        whole(ob.at[c, pl.ds(0, 31)], back_sem.at[c]).wait()

    @pl.when(is_extra)
    def _():
        whole(ob.at[2, pl.ds(0, 31)], back_sem.at[2]).wait()

    @pl.when(has_up)
    def _():
        u_copy().wait_send()
        up_copy().wait_send()
        down_copy().wait_recv()

    @pl.when(has_down)
    def _():
        down_copy().wait_send()
        u_copy().wait_recv()
        up_copy().wait_recv()


def update_kernel(
    sg, above, below, ub, rd, ru,
    sig_out, new_out,
    km, sf, es_h, es_l, el_h, el_l,
):
    row48 = lax.broadcasted_iota(jnp.int32, (48, 128), 0)
    lane48 = lax.broadcasted_iota(jnp.int32, (48, 128), 1)
    lane8 = lax.broadcasted_iota(jnp.int32, (8, 128), 1)
    lane24 = lax.broadcasted_iota(jnp.int32, (24, 128), 1)
    zero48 = jnp.zeros((80, 128), F32)
    zero32 = jnp.zeros((32, 128), F32)
    inside48 = lane48 < B

    def to_rows(u0, u1, u2, lane):
        r1 = jnp.where(lane < 32, pltpu.roll(u0, 32, 1), pltpu.roll(u1, 32, 1))
        r2 = jnp.where(lane < 64, pltpu.roll(u1, 64, 1), pltpu.roll(u2, 64, 1))
        return u0, r1, r2, pltpu.roll(u2, 96, 1)

    def to_tiles(r0, r1, r2, r3, lane):
        m1, m2, m3 = pltpu.roll(r1, 96, 1), pltpu.roll(r2, 64, 1), pltpu.roll(r3, 32, 1)
        return jnp.where(lane < 96, r0, m1), jnp.where(lane < 64, m1, m2), jnp.where(lane < 32, m2, m3)

    def store_pair(high, low, index, re, im):
        re = jnp.concatenate([re, zero32], 0)
        im = jnp.concatenate([im, zero32], 0)
        rh, rl = split(re)
        mh, ml = split(im)
        for ref, r, m in ((high, rh, mh), (low, rl, ml)):
            ref[index, 0:128, 0:128] = r
            ref[index, 0:128, 128:256] = m
            ref[index, 128:256, 0:128] = -m
            ref[index, 128:256, 128:256] = r

    for array in range(4):
        def take(t, array=array):
            return sg[array, t] if array < 2 else (above[t] if array == 2 else below[t])

        def rows(q, carry, array=array, take=take):
            for j, r in enumerate(to_rows(take(3 * q), take(3 * q + 1), take(3 * q + 2), lane8)):
                km[pl.ds(array * 384 + 4 * q + j, 8, stride=48), :] = r
            return carry

        lax.fori_loop(0, 12, rows, 0)

    def flat_store(re, im, out, blk):
        for part, x in ((0, re), (1, im)):
            sf[part] = x
        for part in range(2):
            tiles = to_tiles(*(sf[part, pl.ds(j, 24, stride=4), :] for j in range(4)), lane24)
            for j in range(3):
                out[blk, pl.ds(2 * j + part, 24, stride=6), :] = tiles[j]

    def unpack(index, carry):
        array = index // 4
        e = index % 4
        base = array * 384 + 2 * e * 48
        kr = km[pl.ds(pl.multiple_of(base, 8), 48), :]
        ki = km[pl.ds(pl.multiple_of(base + 48, 8), 48), :]
        krt = -jnp.concatenate([kr, zero48], 0).T
        kit = jnp.concatenate([ki, zero48], 0).T
        less, same = lane48 < row48, lane48 == row48
        top_r = jnp.where(less, krt[:48], jnp.where(same, 0.0, kr))
        top_i = jnp.where(less, kit[:48], ki)
        in_r = jnp.where(less, kr, jnp.where(same, 0.0, krt[:48]))
        in_i = jnp.where(less, ki, jnp.where(same, kr, kit[:48]))
        low_r = jnp.where(lane48 < 48, krt[48:96], pltpu.roll(in_r, 48, 1))
        low_i = jnp.where(lane48 < 48, kit[48:96], pltpu.roll(in_i, 48, 1))
        re = jnp.concatenate([jnp.where(inside48, top_r, 0.0), jnp.where(inside48, low_r, 0.0)], 0)
        im = jnp.concatenate([jnp.where(inside48, top_i, 0.0), jnp.where(inside48, low_i, 0.0)], 0)
        store_pair(es_h, es_l, index, re, im)

        @pl.when(index < 8)
        def _():
            flat_store(re, im, sig_out, index)

        return carry

    lax.fori_loop(0, 16, unpack, 0)

    lane96 = lax.broadcasted_iota(jnp.int32, (96, 128), 1)

    def matrix(source, blk, part):
        u = [source[blk, pl.ds(2 * j + part, 24, stride=6), :] for j in range(3)]
        for j, r in enumerate(to_rows(*u, lane24)):
            sf[part, pl.ds(j, 24, stride=4), :] = r
        return jnp.where(lane96 < B, sf[part], 0.0)

    def flip(x):
        return jnp.concatenate([x, zero32], 0).T[:96]

    def diag_prep(blk, carry):
        store_pair(el_h, el_l, blk, matrix(rd, blk, 0), matrix(rd, blk, 1))
        return carry

    def upper_prep(blk, carry):
        re, im = matrix(ru, blk, 0), matrix(ru, blk, 1)
        store_pair(el_h, el_l, 8 + blk, re, im)

        @pl.when(blk < 4)
        def _():
            store_pair(el_h, el_l, 20 + blk, flip(re), flip(im))

        return carry

    def below_prep(blk, carry):
        store_pair(el_h, el_l, 16 + blk, flip(matrix(ub, blk, 0)), flip(matrix(ub, blk, 1)))
        return carry

    lax.fori_loop(0, 8, diag_prep, 0)
    lax.fori_loop(0, 8, upper_prep, 0)
    lax.fori_loop(0, 4, below_prep, 0)

    transposed = (((1,), (1,)), ((), ()))

    def term(left, middle):
        x = dot3(el_h[left, 0:96, :], el_l[left, 0:96, :], es_h[middle], es_l[middle])
        xh, xl = split(x)
        return dot3(xh, xl, el_h[left], el_l[left], transposed)

    def combine(blk, carry):
        c = blk // 4
        e = blk % 4
        low = jnp.where(c == 0, 12 + e, e)
        high = jnp.where(c == 0, 4 + e, 8 + e)
        total = term(blk, blk) + term(16 + blk, low) + term(8 + blk, high)
        flat_store(total[:, :128], total[:, 128:], new_out, blk)
        return carry

    lax.fori_loop(0, 8, combine, 0)


def flat_view(x):
    return x.reshape(8, 2, 72, 128).transpose(0, 2, 1, 3).reshape(8, 144, 128)


def from_flat(y):
    return y.reshape(8, 72, 2, 128).transpose(0, 2, 1, 3).reshape(2, 4, 2, B * B)


def shards(glesser, wlesser, gret_diag, gret_upper):
    g, w, rd, ru = (flat_view(x) for x in (glesser, wlesser, gret_diag, gret_upper))
    forward, inverse = transforms()
    constants = [jnp.asarray(x) for x in (*two_terms(forward), *two_terms(inverse))]
    vmem = pl.BlockSpec(memory_space=pltpu.VMEM)
    hbm = pl.BlockSpec(memory_space=pl.ANY)
    dma = pltpu.SemaphoreType.DMA
    sg, above, below, ub = pl.pallas_call(
        exchange_kernel,
        out_shape=[
            jax.ShapeDtypeStruct((2, HALF, 8, 128), F32),
            jax.ShapeDtypeStruct((HALF, 8, 128), F32),
            jax.ShapeDtypeStruct((HALF, 8, 128), F32),
            jax.ShapeDtypeStruct((4, 144, 128), F32),
        ],
        in_specs=[hbm] * 3 + [vmem] * 4,
        out_specs=[vmem] * 4,
        scratch_shapes=[
            pltpu.VMEM((8, 160, 128), F32),
            pltpu.VMEM((8, 160, 128), F32),
            pltpu.VMEM((2, 640, 128), F32),
            pltpu.VMEM((3, PEERS, 16, 128), F32),
            pltpu.VMEM((3, PEERS, 8, 128), F32),
            dma((2, 2)), dma((2,)), dma((2,)), dma((2, 4)), dma((3,)), dma((3,)), dma((2,)), dma((2,)), dma((3,)), dma((3,)),
        ],
        compiler_params=pltpu.CompilerParams(collective_id=0, has_side_effects=True, vmem_limit_bytes=VMEM_LIMIT),
        name="exchange",
    )(g, w, ru, *constants)
    sigma, new = pl.pallas_call(
        update_kernel,
        out_shape=[jax.ShapeDtypeStruct((8, 144, 128), F32)] * 2,
        in_specs=[vmem] * 6,
        out_specs=[vmem] * 2,
        scratch_shapes=[
            pltpu.VMEM((4 * 384, 128), F32),
            pltpu.VMEM((2, 96, 128), F32),
            pltpu.VMEM((16, 256, 256), BF16),
            pltpu.VMEM((16, 256, 256), BF16),
            pltpu.VMEM((24, 256, 256), BF16),
            pltpu.VMEM((24, 256, 256), BF16),
        ],
        compiler_params=pltpu.CompilerParams(vmem_limit_bytes=VMEM_LIMIT),
        name="update",
    )(sg, above, below, ub, rd, ru)
    return from_flat(sigma), from_flat(new)


def solution(mesh):
    spec = P("cell", "energy", None, None)
    return jax.shard_map(shards, mesh=mesh, in_specs=(spec,) * 4, out_specs=(spec,) * 2, check_vma=False)
```

```python
import functools

import jax
import jax.numpy as jnp
import ml_dtypes
import numpy as np
from jax import lax
from jax.experimental import pallas as pl
from jax.experimental.pallas import tpu as pltpu
from jax.sharding import PartitionSpec as P

MESH = pl.DeviceIdType.MESH
B = 96
NE = 128
PEERS = 32
HALF = 36
F32 = jnp.float32
BF16 = jnp.bfloat16
VMEM_LIMIT = 56 * 1024 * 1024


def two_terms(x):
    high = x.astype(ml_dtypes.bfloat16)
    return high, (x - high.astype(np.float64)).astype(ml_dtypes.bfloat16)


def transforms():
    n = np.arange(NE)
    k = np.arange(NE)
    angle = 2.0 * np.pi / (4 * NE) * ((n[None, :] * (1 - 4 * k[:, None])) % (4 * NE))
    forward = np.zeros((2, 2, NE, NE, 2))
    inverse = np.zeros((NE, 2, 2, 2, NE))
    scale = NE ** -0.5 / NE
    for part in range(2):
        forward[part, 0, :, :, part] = np.cos(angle)
        forward[part, 1, :, :, part] = np.sin(angle)
        inverse[:, part, part, 0, :] = np.cos(angle).T * scale
        inverse[:, part, part, 1, :] = np.sin(angle).T * scale
    return forward.reshape(512, 256), inverse.reshape(256, 512)


def split(x):
    high = x.astype(BF16)
    return high, (x - high.astype(F32)).astype(BF16)


def dot3(ah, al, bh, bl, dims=(((1,), (0,)), ((), ()))):
    d = functools.partial(lax.dot_general, dimension_numbers=dims, preferred_element_type=F32)
    return d(ah, bh) + (d(al, bh) + d(ah, bl))


def whole(ref, sem):
    return pltpu.make_async_copy(ref, ref, sem)


def kernel(
    g_hbm, w_hbm, rd_hbm, u_hbm, fh, fl, ih, il,
    sig_out, new_out,
    gv, wv, pk, rv, ob, sg, above, below, ub, rd, ru, km, sf, es_h, es_l, el_h, el_l, total,
    load_sem, ret_sem, send_sem, xsend_sem, recv_sem, back_sem, sig_sem, hop_send, hop_recv,
):
    me = lax.axis_index("energy")
    k = lax.axis_index("cell")
    my_z = me // 4
    my_i = my_z // 2
    my_c = my_z % 2
    is_extra = jnp.equal(me % 4, my_i)
    has_up = k < 7
    has_down = k > 0

    for c in range(2):
        pltpu.make_async_copy(g_hbm.at[pl.ds(4 * c, 4)], gv.at[pl.ds(4 * c, 4), pl.ds(0, 144)], load_sem.at[c, 0]).start()
        pltpu.make_async_copy(w_hbm.at[pl.ds(4 * c, 4)], wv.at[pl.ds(4 * c, 4), pl.ds(0, 144)], load_sem.at[c, 1]).start()

    load_rd = pltpu.make_async_copy(rd_hbm, rd, ret_sem.at[0])
    load_ru = pltpu.make_async_copy(u_hbm, ru, ret_sem.at[1])
    load_rd.start()
    load_ru.start()

    barrier = pltpu.get_barrier_semaphore()

    def greet(i, carry):
        pl.semaphore_signal(barrier, inc=1, device_id={"energy": lax.rem(me + i, PEERS)}, device_id_type=MESH)
        return carry

    lax.fori_loop(1, PEERS, greet, 0)

    @pl.when(has_up)
    def _():
        pl.semaphore_signal(barrier, inc=1, device_id={"cell": k + 1}, device_id_type=MESH)

    @pl.when(has_down)
    def _():
        pl.semaphore_signal(barrier, inc=1, device_id={"cell": k - 1}, device_id_type=MESH)

    row = lax.broadcasted_iota(jnp.int32, (40, 128), 0)
    lane = lax.broadcasted_iota(jnp.int32, (40, 128), 1)
    slot_index = row * 128 + lane
    a_index = (slot_index * 43691) >> 22
    b_index = slot_index - a_index * B
    direct = b_index >= a_index
    diagonal = b_index == a_index
    near = lane >= 48

    def pack(c):
        for which, source in enumerate((gv, wv)):
            pltpu.make_async_copy(
                (g_hbm, w_hbm)[which].at[pl.ds(4 * c, 4)], source.at[pl.ds(4 * c, 4), pl.ds(0, 144)], load_sem.at[c, which]
            ).wait()

            def one(e, carry):
                blk = 4 * c + e
                first, far = [], []
                for part in range(2):
                    first.append(source[blk, pl.ds(part, 40, stride=2), :])
                    here = source[blk, pl.ds(72 + part, 40, stride=2), :]
                    after = source[blk, pl.ds(74 + part, 40, stride=2), :]
                    far.append(pltpu.roll(jnp.where(near, here, after), 80, 1))
                re = jnp.where(direct, first[0], far[0])
                re = jnp.where(diagonal, far[1], re)
                im = jnp.where(direct, first[1], far[1])
                base = which * 8 + 2 * e
                pk[c, pl.ds(base, 40, stride=16), :] = re
                pk[c, pl.ds(base + 1, 40, stride=16), :] = im
                return carry

            lax.fori_loop(0, 4, one, 0)

    def outgoing(c, p):
        return pltpu.make_async_remote_copy(
            src_ref=pk.at[c, pl.ds(p * 16, 16)], dst_ref=rv.at[c, me], send_sem=send_sem.at[c], recv_sem=recv_sem.at[c],
            device_id={"energy": p}, device_id_type=MESH,
        )

    def extra_out(c, i):
        return pltpu.make_async_remote_copy(
            src_ref=pk.at[c, pl.ds((PEERS + i) * 16, 16)], dst_ref=rv.at[2, me], send_sem=xsend_sem.at[c, i],
            recv_sem=recv_sem.at[2], device_id={"energy": 4 * (2 * i + c) + i}, device_id_type=MESH,
        )

    def send(c):
        def start(i, carry):
            outgoing(c, lax.rem(me + i, PEERS)).start()
            return carry

        pltpu.make_async_copy(pk.at[c, pl.ds(me * 16, 16)], rv.at[c, me], recv_sem.at[c]).start()
        lax.fori_loop(1, PEERS, start, 0)
        for i in range(4):
            mine = jnp.equal(me, 4 * (2 * i + c) + i)

            @pl.when(jnp.logical_not(mine))
            def _(i=i):
                extra_out(c, i).start()

            @pl.when(mine)
            def _(i=i):
                pltpu.make_async_copy(pk.at[c, pl.ds((PEERS + i) * 16, 16)], rv.at[2, me], recv_sem.at[2]).start()

    pack(0)
    pl.semaphore_wait(barrier, 31 + has_up.astype(jnp.int32) + has_down.astype(jnp.int32))
    send(0)
    pack(1)
    send(1)

    def u_copy():
        return pltpu.make_async_remote_copy(
            src_ref=u_hbm.at[pl.ds(4, 4)], dst_ref=ub, send_sem=hop_send.at[0], recv_sem=hop_recv.at[0],
            device_id={"cell": k + 1}, device_id_type=MESH,
        )

    def down_copy():
        return pltpu.make_async_remote_copy(
            src_ref=sg.at[0], dst_ref=above, send_sem=hop_send.at[1], recv_sem=hop_recv.at[1],
            device_id={"cell": k - 1}, device_id_type=MESH,
        )

    def up_copy():
        return pltpu.make_async_remote_copy(
            src_ref=sg.at[1], dst_ref=below, send_sem=hop_send.at[2], recv_sem=hop_recv.at[2],
            device_id={"cell": k + 1}, device_id_type=MESH,
        )

    @pl.when(has_up)
    def _():
        u_copy().start()

    @pl.when(jnp.logical_not(has_up))
    def _():
        above[...] = jnp.zeros_like(above)

    @pl.when(jnp.logical_not(has_down))
    def _():
        below[...] = jnp.zeros_like(below)
        ub[...] = jnp.zeros_like(ub)

    def back(slot, c, tile, p):
        return pltpu.make_async_remote_copy(
            src_ref=ob.at[slot, p], dst_ref=sg.at[c, tile], send_sem=back_sem.at[slot], recv_sem=sig_sem.at[c],
            device_id={"energy": p}, device_id_type=MESH,
        )

    def convolve(slot, c, tile):
        whole(rv.at[slot], recv_sem.at[slot]).wait()
        green = rv[slot, :, 0:8, :].reshape(256, 128)
        screen = rv[slot, :, 8:16, :].reshape(256, 128)
        xh, xl = split(jnp.concatenate([green, screen], 1))
        hat = dot3(fh[...], fl[...], xh, xl)
        xr, xi, yr, yi = (hat[128 * j:128 * j + 128] for j in range(4))
        xrg, xrw, xig, xiw = xr[:, :128], xr[:, 128:], xi[:, :128], xi[:, 128:]
        yrg, yrw, yig, yiw = yr[:, :128], yr[:, 128:], yi[:, :128], yi[:, 128:]
        xx_r = xrg * xrw - xig * xiw
        xx_i = xrg * xiw + xig * xrw
        yy_r = yrg * yrw - yig * yiw
        yy_i = yrg * yiw + yig * yrw
        xy_r = (xrg * yrw - xig * yiw) + (yrg * xrw - yig * xiw)
        xy_i = (xrg * yiw + xig * yrw) + (yrg * xiw + yig * xrw)
        main = jnp.concatenate([-xy_r, -xy_i, xx_r - yy_r, xx_i - yy_i], 0)
        diag = jnp.concatenate([-xx_r, -xx_i, -yy_r, -yy_i], 0)
        zh, zl = split(jnp.concatenate([main, diag], 1))
        out = dot3(ih[...], il[...], zh, zl)
        position = tile * 128 + lax.broadcasted_iota(jnp.int32, (256, 128), 1)
        on_diagonal = position == ((position * 43241) >> 22) * 97
        ob[slot] = jnp.where(on_diagonal, out[:, 128:], out[:, :128]).reshape(PEERS, 8, 128)

        pltpu.make_async_copy(ob.at[slot, me], sg.at[c, tile], sig_sem.at[c]).start()

        def start(i, carry):
            back(slot, c, tile, lax.rem(me + i, PEERS)).start()
            return carry

        lax.fori_loop(1, PEERS, start, 0)

    row48 = lax.broadcasted_iota(jnp.int32, (48, 128), 0)
    lane48 = lax.broadcasted_iota(jnp.int32, (48, 128), 1)
    lane8 = lax.broadcasted_iota(jnp.int32, (8, 128), 1)
    lane24 = lax.broadcasted_iota(jnp.int32, (24, 128), 1)
    zero48 = jnp.zeros((80, 128), F32)
    zero32 = jnp.zeros((32, 128), F32)
    inside48 = lane48 < B

    def to_rows(u0, u1, u2, lane):
        r1 = jnp.where(lane < 32, pltpu.roll(u0, 32, 1), pltpu.roll(u1, 32, 1))
        r2 = jnp.where(lane < 64, pltpu.roll(u1, 64, 1), pltpu.roll(u2, 64, 1))
        return u0, r1, r2, pltpu.roll(u2, 96, 1)

    def to_tiles(r0, r1, r2, r3, lane):
        m1, m2, m3 = pltpu.roll(r1, 96, 1), pltpu.roll(r2, 64, 1), pltpu.roll(r3, 32, 1)
        return jnp.where(lane < 96, r0, m1), jnp.where(lane < 64, m1, m2), jnp.where(lane < 32, m2, m3)

    def store_pair(high, low, index, re, im):
        re = jnp.concatenate([re, zero32], 0)
        im = jnp.concatenate([im, zero32], 0)
        rh, rl = split(re)
        mh, ml = split(im)
        for ref, r, m in ((high, rh, mh), (low, rl, ml)):
            ref[index, 0:128, 0:128] = r
            ref[index, 0:128, 128:256] = m
            ref[index, 128:256, 0:128] = -m
            ref[index, 128:256, 128:256] = r

    def flat_store(re, im, out, blk):
        for part, x in ((0, re), (1, im)):
            sf[part] = x
        for part in range(2):
            tiles = to_tiles(*(sf[part, pl.ds(j, 24, stride=4), :] for j in range(4)), lane24)
            for j in range(3):
                out[blk, pl.ds(2 * j + part, 24, stride=6), :] = tiles[j]

    def unpack(index, carry):
        array = index // 4
        e = index % 4
        base = array * 384 + 2 * e * 48
        kr = km[pl.ds(pl.multiple_of(base, 8), 48), :]
        ki = km[pl.ds(pl.multiple_of(base + 48, 8), 48), :]
        krt = -jnp.concatenate([kr, zero48], 0).T
        kit = jnp.concatenate([ki, zero48], 0).T
        less, same = lane48 < row48, lane48 == row48
        top_r = jnp.where(less, krt[:48], jnp.where(same, 0.0, kr))
        top_i = jnp.where(less, kit[:48], ki)
        in_r = jnp.where(less, kr, jnp.where(same, 0.0, krt[:48]))
        in_i = jnp.where(less, ki, jnp.where(same, kr, kit[:48]))
        low_r = jnp.where(lane48 < 48, krt[48:96], pltpu.roll(in_r, 48, 1))
        low_i = jnp.where(lane48 < 48, kit[48:96], pltpu.roll(in_i, 48, 1))
        re = jnp.concatenate([jnp.where(inside48, top_r, 0.0), jnp.where(inside48, low_r, 0.0)], 0)
        im = jnp.concatenate([jnp.where(inside48, top_i, 0.0), jnp.where(inside48, low_i, 0.0)], 0)
        store_pair(es_h, es_l, index, re, im)

        @pl.when(index < 8)
        def _():
            flat_store(re, im, sig_out, index)

        return carry

    def to_matrices(array):
        def take(t):
            return sg[array, t] if array < 2 else (above[t] if array == 2 else below[t])

        def rows(q, carry):
            for j, r in enumerate(to_rows(take(3 * q), take(3 * q + 1), take(3 * q + 2), lane8)):
                km[pl.ds(array * 384 + 4 * q + j, 8, stride=48), :] = r
            return carry

        lax.fori_loop(0, 12, rows, 0)
        lax.fori_loop(4 * array, 4 * array + 4, unpack, 0)

    lane96 = lax.broadcasted_iota(jnp.int32, (96, 128), 1)

    def matrix(source, blk, part):
        u = [source[blk, pl.ds(2 * j + part, 24, stride=6), :] for j in range(3)]
        for j, r in enumerate(to_rows(*u, lane24)):
            sf[part, pl.ds(j, 24, stride=4), :] = r
        return jnp.where(lane96 < B, sf[part], 0.0)

    def flip(x):
        return jnp.concatenate([x, zero32], 0).T[:96]

    def diag_prep(blk, carry):
        store_pair(el_h, el_l, blk, matrix(rd, blk, 0), matrix(rd, blk, 1))
        return carry

    def upper_prep(blk, carry):
        re, im = matrix(ru, blk, 0), matrix(ru, blk, 1)
        store_pair(el_h, el_l, 8 + blk, re, im)

        @pl.when(blk < 4)
        def _():
            store_pair(el_h, el_l, 20 + blk, flip(re), flip(im))

        return carry

    def below_prep(blk, carry):
        store_pair(el_h, el_l, 16 + blk, flip(matrix(ub, blk, 0)), flip(matrix(ub, blk, 1)))
        return carry

    transposed = (((1,), (1,)), ((), ()))

    def term(left, middle):
        x = dot3(el_h[left, 0:96, :], el_l[left, 0:96, :], es_h[middle], es_l[middle])
        xh, xl = split(x)
        return dot3(xh, xl, el_h[left], el_l[left], transposed)

    def add_terms(*pairs):
        def one(e, carry):
            for blk, left, middle, first in pairs:
                value = term(left + e, middle + e)
                if first:
                    total[blk + e] = value
                else:
                    total[blk + e] += value
            return carry

        lax.fori_loop(0, 4, one, 0)

    def finish(c):
        def one(blk, carry):
            flat_store(total[blk, :, :128], total[blk, :, 128:], new_out, blk)
            return carry

        lax.fori_loop(4 * c, 4 * c + 4, one, 0)

    def convolve_cell(c):
        def step(j, inner):
            slot = jnp.where(j == 0, c, 2)
            tile = jnp.where(j == 0, me, PEERS + my_i)
            convolve(slot, c, tile)
            return inner

        lax.fori_loop(0, 1 + jnp.where(jnp.logical_and(is_extra, my_c == c), 1, 0), step, 0)

    load_rd.wait()
    lax.fori_loop(0, 8, diag_prep, 0)
    convolve_cell(0)
    load_ru.wait()
    lax.fori_loop(0, 8, upper_prep, 0)
    convolve_cell(1)

    @pl.when(has_down)
    def _():
        u_copy().wait_recv()

    lax.fori_loop(0, 4, below_prep, 0)

    whole(sg.at[0], sig_sem.at[0]).wait()

    @pl.when(has_down)
    def _():
        down_copy().start()

    to_matrices(0)
    add_terms((0, 0, 0, True), (4, 20, 0, True))

    @pl.when(has_up)
    def _():
        down_copy().wait_recv()

    to_matrices(2)
    add_terms((4, 12, 8, False))
    whole(sg.at[1], sig_sem.at[1]).wait()

    @pl.when(has_up)
    def _():
        up_copy().start()

    to_matrices(1)
    add_terms((4, 4, 4, False), (0, 8, 4, False))
    finish(1)

    @pl.when(has_down)
    def _():
        up_copy().wait_recv()

    to_matrices(3)
    add_terms((0, 16, 12, False))
    finish(0)

    for c in range(2):
        whole(pk.at[c, pl.ds(0, 31 * 16)], send_sem.at[c]).wait()
        for i in range(4):
            @pl.when(jnp.logical_not(jnp.equal(me, 4 * (2 * i + c) + i)))
            def _(c=c, i=i):
                extra_out(c, i).wait_send()
        whole(ob.at[c, pl.ds(0, 31)], back_sem.at[c]).wait()

    @pl.when(is_extra)
    def _():
        whole(ob.at[2, pl.ds(0, 31)], back_sem.at[2]).wait()

    @pl.when(has_up)
    def _():
        u_copy().wait_send()
        up_copy().wait_send()

    @pl.when(has_down)
    def _():
        down_copy().wait_send()


def flat_view(x):
    return x.reshape(8, 2, 72, 128).transpose(0, 2, 1, 3).reshape(8, 144, 128)


def from_flat(y):
    return y.reshape(8, 72, 2, 128).transpose(0, 2, 1, 3).reshape(2, 4, 2, B * B)


def shards(glesser, wlesser, gret_diag, gret_upper):
    g, w, rd, ru = (flat_view(x) for x in (glesser, wlesser, gret_diag, gret_upper))
    forward, inverse = transforms()
    constants = [jnp.asarray(x) for x in (*two_terms(forward), *two_terms(inverse))]
    vmem = pl.BlockSpec(memory_space=pltpu.VMEM)
    hbm = pl.BlockSpec(memory_space=pl.ANY)
    dma = pltpu.SemaphoreType.DMA
    sigma, new = pl.pallas_call(
        kernel,
        out_shape=[jax.ShapeDtypeStruct((8, 144, 128), F32)] * 2,
        in_specs=[hbm] * 4 + [vmem] * 4,
        out_specs=[vmem] * 2,
        scratch_shapes=[
            pltpu.VMEM((8, 160, 128), F32),
            pltpu.VMEM((8, 160, 128), F32),
            pltpu.VMEM((2, 640, 128), F32),
            pltpu.VMEM((3, PEERS, 16, 128), F32),
            pltpu.VMEM((3, PEERS, 8, 128), F32),
            pltpu.VMEM((2, HALF, 8, 128), F32),
            pltpu.VMEM((HALF, 8, 128), F32),
            pltpu.VMEM((HALF, 8, 128), F32),
            pltpu.VMEM((4, 144, 128), F32),
            pltpu.VMEM((8, 144, 128), F32),
            pltpu.VMEM((8, 144, 128), F32),
            pltpu.VMEM((4 * 384, 128), F32),
            pltpu.VMEM((2, 96, 128), F32),
            pltpu.VMEM((16, 256, 256), BF16),
            pltpu.VMEM((16, 256, 256), BF16),
            pltpu.VMEM((24, 256, 256), BF16),
            pltpu.VMEM((24, 256, 256), BF16),
            pltpu.VMEM((8, 96, 256), F32),
            dma((2, 2)), dma((2,)), dma((2,)), dma((2, 4)), dma((3,)), dma((3,)), dma((2,)), dma((3,)), dma((3,)),
        ],
        compiler_params=pltpu.CompilerParams(collective_id=0, has_side_effects=True, vmem_limit_bytes=VMEM_LIMIT),
        name="update",
    )(g, w, rd, ru, *constants)
    return from_flat(sigma), from_flat(new)


def solution(mesh):
    spec = P("cell", "energy", None, None)
    return jax.shard_map(shards, mesh=mesh, in_specs=(spec,) * 4, out_specs=(spec,) * 2, check_vma=False)
```

```python
import functools

import jax
import jax.numpy as jnp
import ml_dtypes
import numpy as np
from jax import lax
from jax.experimental import pallas as pl
from jax.experimental.pallas import tpu as pltpu
from jax.sharding import PartitionSpec as P

MESH = pl.DeviceIdType.MESH
B = 96
NE = 128
PEERS = 32
HALF = 36
F32 = jnp.float32
BF16 = jnp.bfloat16
PIECES = 4
VMEM_LIMIT = 56 * 1024 * 1024


def two_terms(x):
    high = x.astype(ml_dtypes.bfloat16)
    return high, (x - high.astype(np.float64)).astype(ml_dtypes.bfloat16)


def transforms():
    n = np.arange(NE)
    k = np.arange(NE)
    angle = 2.0 * np.pi / (4 * NE) * ((n[None, :] * (1 - 4 * k[:, None])) % (4 * NE))
    forward = np.zeros((2, 2, NE, NE, 2))
    inverse = np.zeros((NE, 2, 2, 2, NE))
    scale = NE ** -0.5 / NE
    for part in range(2):
        forward[part, 0, :, :, part] = np.cos(angle)
        forward[part, 1, :, :, part] = np.sin(angle)
        inverse[:, part, part, 0, :] = np.cos(angle).T * scale
        inverse[:, part, part, 1, :] = np.sin(angle).T * scale
    return forward.reshape(512, 256), inverse.reshape(256, 512)


def split(x):
    high = x.astype(BF16)
    return high, (x - high.astype(F32)).astype(BF16)


def dot3(ah, al, bh, bl, dims=(((1,), (0,)), ((), ()))):
    d = functools.partial(lax.dot_general, dimension_numbers=dims, preferred_element_type=F32)
    return d(ah, bh) + (d(al, bh) + d(ah, bl))


def whole(ref, sem):
    return pltpu.make_async_copy(ref, ref, sem)


def kernel(
    g_hbm, w_hbm, rd_hbm, u_hbm, fh, fl, ih, il,
    sig_out, new_out,
    gv, wv, pk, rv, ob, sg, above, below, ub, rd, ru, km, sf, es_h, es_l, el_h, el_l, total,
    load_sem, ret_sem, send_sem, xsend_sem, recv_sem, back_sem, sig_sem, hop_send, hop_recv,
):
    me = lax.axis_index("energy")
    k = lax.axis_index("cell")
    my_z = me // 4
    my_i = my_z // 2
    my_c = my_z % 2
    is_extra = jnp.equal(me % 4, my_i)
    has_up = k < 7
    has_down = k > 0

    for c in range(2):
        pltpu.make_async_copy(g_hbm.at[pl.ds(4 * c, 4)], gv.at[pl.ds(4 * c, 4), pl.ds(0, 144)], load_sem.at[c, 0]).start()
        pltpu.make_async_copy(w_hbm.at[pl.ds(4 * c, 4)], wv.at[pl.ds(4 * c, 4), pl.ds(0, 144)], load_sem.at[c, 1]).start()

    load_rd = pltpu.make_async_copy(rd_hbm, rd, ret_sem.at[0])
    load_ru = pltpu.make_async_copy(u_hbm, ru, ret_sem.at[1])
    load_rd.start()
    load_ru.start()

    barrier = pltpu.get_barrier_semaphore()

    def greet(i, carry):
        pl.semaphore_signal(barrier, inc=1, device_id={"energy": lax.rem(me + i, PEERS)}, device_id_type=MESH)
        return carry

    lax.fori_loop(1, PEERS, greet, 0)

    @pl.when(has_up)
    def _():
        pl.semaphore_signal(barrier, inc=1, device_id={"cell": k + 1}, device_id_type=MESH)

    @pl.when(has_down)
    def _():
        pl.semaphore_signal(barrier, inc=1, device_id={"cell": k - 1}, device_id_type=MESH)

    row = lax.broadcasted_iota(jnp.int32, (40, 128), 0)
    lane = lax.broadcasted_iota(jnp.int32, (40, 128), 1)
    slot_index = row * 128 + lane
    a_index = (slot_index * 43691) >> 22
    b_index = slot_index - a_index * B
    direct = b_index >= a_index
    diagonal = b_index == a_index
    near = lane >= 48

    def pack(c):
        for which, source in enumerate((gv, wv)):
            pltpu.make_async_copy(
                (g_hbm, w_hbm)[which].at[pl.ds(4 * c, 4)], source.at[pl.ds(4 * c, 4), pl.ds(0, 144)], load_sem.at[c, which]
            ).wait()

            def one(e, carry):
                blk = 4 * c + e
                first, far = [], []
                for part in range(2):
                    first.append(source[blk, pl.ds(part, 40, stride=2), :])
                    here = source[blk, pl.ds(72 + part, 40, stride=2), :]
                    after = source[blk, pl.ds(74 + part, 40, stride=2), :]
                    far.append(pltpu.roll(jnp.where(near, here, after), 80, 1))
                re = jnp.where(direct, first[0], far[0])
                re = jnp.where(diagonal, far[1], re)
                im = jnp.where(direct, first[1], far[1])
                base = which * 8 + 2 * e
                pk[c, pl.ds(base, 40, stride=16), :] = re
                pk[c, pl.ds(base + 1, 40, stride=16), :] = im
                return carry

            lax.fori_loop(0, 4, one, 0)

    def outgoing(c, p):
        return pltpu.make_async_remote_copy(
            src_ref=pk.at[c, pl.ds(p * 16, 16)], dst_ref=rv.at[c, me], send_sem=send_sem.at[c], recv_sem=recv_sem.at[c],
            device_id={"energy": p}, device_id_type=MESH,
        )

    def extra_out(c, i):
        return pltpu.make_async_remote_copy(
            src_ref=pk.at[c, pl.ds((PEERS + i) * 16, 16)], dst_ref=rv.at[2, me], send_sem=xsend_sem.at[c, i],
            recv_sem=recv_sem.at[2], device_id={"energy": 4 * (2 * i + c) + i}, device_id_type=MESH,
        )

    def send(c):
        def start(i, carry):
            outgoing(c, lax.rem(me + i, PEERS)).start()
            return carry

        pltpu.make_async_copy(pk.at[c, pl.ds(me * 16, 16)], rv.at[c, me], recv_sem.at[c]).start()
        lax.fori_loop(1, PEERS, start, 0)
        for i in range(4):
            mine = jnp.equal(me, 4 * (2 * i + c) + i)

            @pl.when(jnp.logical_not(mine))
            def _(i=i):
                extra_out(c, i).start()

            @pl.when(mine)
            def _(i=i):
                pltpu.make_async_copy(pk.at[c, pl.ds((PEERS + i) * 16, 16)], rv.at[2, me], recv_sem.at[2]).start()

    pack(0)
    pl.semaphore_wait(barrier, 31 + has_up.astype(jnp.int32) + has_down.astype(jnp.int32))
    send(0)
    pack(1)
    send(1)

    def u_copy():
        return pltpu.make_async_remote_copy(
            src_ref=u_hbm.at[pl.ds(4, 4)], dst_ref=ub, send_sem=hop_send.at[0], recv_sem=hop_recv.at[0],
            device_id={"cell": k + 1}, device_id_type=MESH,
        )

    def down_copy():
        return pltpu.make_async_remote_copy(
            src_ref=sg.at[0], dst_ref=above, send_sem=hop_send.at[1], recv_sem=hop_recv.at[1],
            device_id={"cell": k - 1}, device_id_type=MESH,
        )

    def up_copy():
        return pltpu.make_async_remote_copy(
            src_ref=sg.at[1], dst_ref=below, send_sem=hop_send.at[2], recv_sem=hop_recv.at[2],
            device_id={"cell": k + 1}, device_id_type=MESH,
        )

    @pl.when(has_up)
    def _():
        u_copy().start()

    @pl.when(jnp.logical_not(has_up))
    def _():
        above[...] = jnp.zeros_like(above)

    @pl.when(jnp.logical_not(has_down))
    def _():
        below[...] = jnp.zeros_like(below)
        ub[...] = jnp.zeros_like(ub)

    def back(slot, c, tile, p):
        return pltpu.make_async_remote_copy(
            src_ref=ob.at[slot, p], dst_ref=sg.at[c, tile], send_sem=back_sem.at[slot], recv_sem=sig_sem.at[c],
            device_id={"energy": p}, device_id_type=MESH,
        )

    def convolve(slot, c, tile):
        whole(rv.at[slot], recv_sem.at[slot]).wait()
        green = rv[slot, :, 0:8, :].reshape(256, 128)
        screen = rv[slot, :, 8:16, :].reshape(256, 128)
        xh, xl = split(jnp.concatenate([green, screen], 1))
        hat = dot3(fh[...], fl[...], xh, xl)
        xr, xi, yr, yi = (hat[128 * j:128 * j + 128] for j in range(4))
        xrg, xrw, xig, xiw = xr[:, :128], xr[:, 128:], xi[:, :128], xi[:, 128:]
        yrg, yrw, yig, yiw = yr[:, :128], yr[:, 128:], yi[:, :128], yi[:, 128:]
        xx_r = xrg * xrw - xig * xiw
        xx_i = xrg * xiw + xig * xrw
        yy_r = yrg * yrw - yig * yiw
        yy_i = yrg * yiw + yig * yrw
        xy_r = (xrg * yrw - xig * yiw) + (yrg * xrw - yig * xiw)
        xy_i = (xrg * yiw + xig * yrw) + (yrg * xiw + yig * xrw)
        main = jnp.concatenate([-xy_r, -xy_i, xx_r - yy_r, xx_i - yy_i], 0)
        diag = jnp.concatenate([-xx_r, -xx_i, -yy_r, -yy_i], 0)
        zh, zl = split(jnp.concatenate([main, diag], 1))
        out = dot3(ih[...], il[...], zh, zl)
        position = tile * 128 + lax.broadcasted_iota(jnp.int32, (256, 128), 1)
        on_diagonal = position == ((position * 43241) >> 22) * 97
        ob[slot] = jnp.where(on_diagonal, out[:, 128:], out[:, :128]).reshape(PEERS, 8, 128)

        pltpu.make_async_copy(ob.at[slot, me], sg.at[c, tile], sig_sem.at[c]).start()

        def start(i, carry):
            back(slot, c, tile, lax.rem(me + i, PEERS)).start()
            return carry

        lax.fori_loop(1, PEERS, start, 0)

    row48 = lax.broadcasted_iota(jnp.int32, (48, 128), 0)
    lane48 = lax.broadcasted_iota(jnp.int32, (48, 128), 1)
    lane8 = lax.broadcasted_iota(jnp.int32, (8, 128), 1)
    lane24 = lax.broadcasted_iota(jnp.int32, (24, 128), 1)
    zero48 = jnp.zeros((80, 128), F32)
    zero32 = jnp.zeros((32, 128), F32)
    inside48 = lane48 < B

    def to_rows(u0, u1, u2, lane):
        r1 = jnp.where(lane < 32, pltpu.roll(u0, 32, 1), pltpu.roll(u1, 32, 1))
        r2 = jnp.where(lane < 64, pltpu.roll(u1, 64, 1), pltpu.roll(u2, 64, 1))
        return u0, r1, r2, pltpu.roll(u2, 96, 1)

    def to_tiles(r0, r1, r2, r3, lane):
        m1, m2, m3 = pltpu.roll(r1, 96, 1), pltpu.roll(r2, 64, 1), pltpu.roll(r3, 32, 1)
        return jnp.where(lane < 96, r0, m1), jnp.where(lane < 64, m1, m2), jnp.where(lane < 32, m2, m3)

    def store_pair(high, low, index, re, im):
        re = jnp.concatenate([re, zero32], 0)
        im = jnp.concatenate([im, zero32], 0)
        rh, rl = split(re)
        mh, ml = split(im)
        for ref, r, m in ((high, rh, mh), (low, rl, ml)):
            ref[index, 0:128, 0:128] = r
            ref[index, 0:128, 128:256] = m
            ref[index, 128:256, 0:128] = -m
            ref[index, 128:256, 128:256] = r

    def flat_store(matrices, out, blk):
        for part in range(2):
            tiles = to_tiles(*(matrices[blk, part, pl.ds(j, 24, stride=4), :] for j in range(4)), lane24)
            for j in range(3):
                out[blk, pl.ds(2 * j + part, 24, stride=6), :] = tiles[j]

    def unpack(index):
        base = 96 * index
        kr = km[base:base + 48, :]
        ki = km[base + 48:base + 96, :]
        krt = -jnp.concatenate([kr, zero48], 0).T
        kit = jnp.concatenate([ki, zero48], 0).T
        less, same = lane48 < row48, lane48 == row48
        top_r = jnp.where(less, krt[:48], jnp.where(same, 0.0, kr))
        top_i = jnp.where(less, kit[:48], ki)
        in_r = jnp.where(less, kr, jnp.where(same, 0.0, krt[:48]))
        in_i = jnp.where(less, ki, jnp.where(same, kr, kit[:48]))
        low_r = jnp.where(lane48 < 48, krt[48:96], pltpu.roll(in_r, 48, 1))
        low_i = jnp.where(lane48 < 48, kit[48:96], pltpu.roll(in_i, 48, 1))
        re = jnp.concatenate([jnp.where(inside48, top_r, 0.0), jnp.where(inside48, low_r, 0.0)], 0)
        im = jnp.concatenate([jnp.where(inside48, top_i, 0.0), jnp.where(inside48, low_i, 0.0)], 0)
        store_pair(es_h, es_l, index, re, im)
        if index < 8:
            sf[index, 0] = re
            sf[index, 1] = im

    def to_matrices(array):
        def take(t):
            return sg[array, t] if array < 2 else (above[t] if array == 2 else below[t])

        for q in range(12):
            for j, r in enumerate(to_rows(take(3 * q), take(3 * q + 1), take(3 * q + 2), lane8)):
                km[pl.ds(array * 384 + 4 * q + j, 8, stride=48), :] = r
        for index in range(4 * array, 4 * array + 4):
            unpack(index)

    lane96 = lax.broadcasted_iota(jnp.int32, (96, 128), 1)

    def matrix(source, blk, part):
        u = [source[blk, pl.ds(2 * j + part, 24, stride=6), :] for j in range(3)]
        for j, r in enumerate(to_rows(*u, lane24)):
            sf[blk, part, pl.ds(j, 24, stride=4), :] = r
        return jnp.where(lane96 < B, sf[blk, part], 0.0)

    def flip(x):
        return jnp.concatenate([x, zero32], 0).T[:96]

    def diag_prep(blk, carry):
        store_pair(el_h, el_l, blk, matrix(rd, blk, 0), matrix(rd, blk, 1))
        return carry

    def upper_prep(blk, carry):
        re, im = matrix(ru, blk, 0), matrix(ru, blk, 1)
        store_pair(el_h, el_l, 8 + blk, re, im)

        @pl.when(blk < 4)
        def _():
            store_pair(el_h, el_l, 20 + blk, flip(re), flip(im))

        return carry

    def below_prep(blk, carry):
        store_pair(el_h, el_l, 16 + blk, flip(matrix(ub, blk, 0)), flip(matrix(ub, blk, 1)))
        return carry

    transposed = (((1,), (1,)), ((), ()))

    def add_terms(middle, pairs):
        for e in range(4):
            left_h = jnp.concatenate([el_h[left + e, 0:96, :] for _, left, _ in pairs], 0)
            left_l = jnp.concatenate([el_l[left + e, 0:96, :] for _, left, _ in pairs], 0)
            xh, xl = split(dot3(left_h, left_l, es_h[middle + e], es_l[middle + e]))
            for i, (blk, left, first) in enumerate(pairs):
                rows = slice(96 * i, 96 * i + 96)
                value = dot3(xh[rows], xl[rows], el_h[left + e], el_l[left + e], transposed)
                for part in range(2):
                    half = value[:, 128 * part:128 * part + 128]
                    if first:
                        total[blk + e, part] = half
                    else:
                        total[blk + e, part] += half

    def finish(c):
        for blk in range(4 * c, 4 * c + 4):
            flat_store(total, new_out, blk)

    def sigma_flat():
        for blk in range(8):
            flat_store(sf, sig_out, blk)

    def convolve_cell(c):
        def step(j, inner):
            slot = jnp.where(j == 0, c, 2)
            tile = jnp.where(j == 0, me, PEERS + my_i)
            convolve(slot, c, tile)
            return inner

        lax.fori_loop(0, 1 + jnp.where(jnp.logical_and(is_extra, my_c == c), 1, 0), step, 0)

    load_rd.wait()
    lax.fori_loop(0, 8, diag_prep, 0)
    convolve_cell(0)
    load_ru.wait()
    lax.fori_loop(0, 8, upper_prep, 0)
    convolve_cell(1)

    @pl.when(has_down)
    def _():
        u_copy().wait_recv()

    lax.fori_loop(0, 4, below_prep, 0)

    whole(sg.at[0], sig_sem.at[0]).wait()

    @pl.when(has_down)
    def _():
        down_copy().start()

    to_matrices(0)
    add_terms(0, ((0, 0, True), (4, 20, True)))
    whole(sg.at[1], sig_sem.at[1]).wait()

    @pl.when(has_up)
    def _():
        up_copy().start()

    to_matrices(1)
    add_terms(4, ((4, 4, False), (0, 8, False)))

    @pl.when(has_up)
    def _():
        down_copy().wait_recv()

    to_matrices(2)
    add_terms(8, ((4, 12, False),))
    finish(1)
    sigma_flat()

    @pl.when(has_down)
    def _():
        up_copy().wait_recv()

    to_matrices(3)
    add_terms(12, ((0, 16, False),))
    finish(0)

    for c in range(2):
        whole(pk.at[c, pl.ds(0, 31 * 16)], send_sem.at[c]).wait()
        for i in range(4):
            @pl.when(jnp.logical_not(jnp.equal(me, 4 * (2 * i + c) + i)))
            def _(c=c, i=i):
                extra_out(c, i).wait_send()
        whole(ob.at[c, pl.ds(0, 31)], back_sem.at[c]).wait()

    @pl.when(is_extra)
    def _():
        whole(ob.at[2, pl.ds(0, 31)], back_sem.at[2]).wait()

    @pl.when(has_up)
    def _():
        u_copy().wait_send()
        up_copy().wait_send()

    @pl.when(has_down)
    def _():
        down_copy().wait_send()


def publish_kernel(a, b, a_out, b_out, sems):
    copies = []
    for i, (src, dst) in enumerate(((a, a_out), (b, b_out))):
        for j in range(PIECES):
            part = pl.ds(j * (8 // PIECES), 8 // PIECES)
            copies.append(pltpu.make_async_copy(src.at[part], dst.at[part], sems.at[i, j]))
    for copy in copies:
        copy.start()
    for copy in copies:
        copy.wait()


def flat_view(x):
    return x.reshape(8, 2, 72, 128).transpose(0, 2, 1, 3).reshape(8, 144, 128)


def from_flat(y):
    return y.reshape(8, 72, 2, 128).transpose(0, 2, 1, 3).reshape(2, 4, 2, B * B)


def shards(glesser, wlesser, gret_diag, gret_upper):
    g, w, rd, ru = (flat_view(x) for x in (glesser, wlesser, gret_diag, gret_upper))
    forward, inverse = transforms()
    constants = [jnp.asarray(x) for x in (*two_terms(forward), *two_terms(inverse))]
    vmem = pl.BlockSpec(memory_space=pltpu.VMEM)
    hbm = pl.BlockSpec(memory_space=pl.ANY)
    dma = pltpu.SemaphoreType.DMA
    sigma, new = pl.pallas_call(
        kernel,
        out_shape=[pltpu.VMEM((8, 144, 128), F32)] * 2,
        in_specs=[hbm] * 4 + [vmem] * 4,
        out_specs=[vmem] * 2,
        scratch_shapes=[
            pltpu.VMEM((8, 160, 128), F32),
            pltpu.VMEM((8, 160, 128), F32),
            pltpu.VMEM((2, 640, 128), F32),
            pltpu.VMEM((3, PEERS, 16, 128), F32),
            pltpu.VMEM((3, PEERS, 8, 128), F32),
            pltpu.VMEM((2, HALF, 8, 128), F32),
            pltpu.VMEM((HALF, 8, 128), F32),
            pltpu.VMEM((HALF, 8, 128), F32),
            pltpu.VMEM((4, 144, 128), F32),
            pltpu.VMEM((8, 144, 128), F32),
            pltpu.VMEM((8, 144, 128), F32),
            pltpu.VMEM((4 * 384, 128), F32),
            pltpu.VMEM((8, 2, 96, 128), F32),
            pltpu.VMEM((16, 256, 256), BF16),
            pltpu.VMEM((16, 256, 256), BF16),
            pltpu.VMEM((24, 256, 256), BF16),
            pltpu.VMEM((24, 256, 256), BF16),
            pltpu.VMEM((8, 2, 96, 128), F32),
            dma((2, 2)), dma((2,)), dma((2,)), dma((2, 4)), dma((3,)), dma((3,)), dma((2,)), dma((3,)), dma((3,)),
        ],
        compiler_params=pltpu.CompilerParams(collective_id=0, has_side_effects=True, vmem_limit_bytes=VMEM_LIMIT),
        name="update",
    )(g, w, rd, ru, *constants)
    sigma, new = pl.pallas_call(
        publish_kernel,
        out_shape=[jax.ShapeDtypeStruct((8, 144, 128), F32)] * 2,
        in_specs=[vmem] * 2,
        out_specs=[hbm] * 2,
        scratch_shapes=[dma((2, PIECES))],
        name="publish",
    )(*(pltpu.with_memory_space_constraint(x, pltpu.VMEM) for x in (sigma, new)))
    return from_flat(sigma), from_flat(new)


def solution(mesh):
    spec = P("cell", "energy", None, None)
    return jax.shard_map(shards, mesh=mesh, in_specs=(spec,) * 4, out_specs=(spec,) * 2, check_vma=False)
```

```python
import functools

import jax
import jax.numpy as jnp
import ml_dtypes
import numpy as np
from jax import lax
from jax.experimental import pallas as pl
from jax.experimental.pallas import tpu as pltpu
from jax.sharding import PartitionSpec as P

MESH = pl.DeviceIdType.MESH
B = 96
NE = 128
PEERS = 32
HALF = 36
F32 = jnp.float32
BF16 = jnp.bfloat16
PIECES = 4
VMEM_LIMIT = 56 * 1024 * 1024


def two_terms(x):
    high = x.astype(ml_dtypes.bfloat16)
    return high, (x - high.astype(np.float64)).astype(ml_dtypes.bfloat16)


def transforms():
    n = np.arange(NE)
    k = np.arange(NE)
    angle = 2.0 * np.pi / (4 * NE) * ((n[None, :] * (1 - 4 * k[:, None])) % (4 * NE))
    forward = np.zeros((2, 2, NE, NE, 2))
    inverse = np.zeros((NE, 2, 2, 2, NE))
    scale = NE ** -0.5 / NE
    for part in range(2):
        forward[part, 0, :, :, part] = np.cos(angle)
        forward[part, 1, :, :, part] = np.sin(angle)
        inverse[:, part, part, 0, :] = np.cos(angle).T * scale
        inverse[:, part, part, 1, :] = np.sin(angle).T * scale
    return forward.reshape(512, 256), inverse.reshape(256, 512)


def split(x):
    high = x.astype(BF16)
    return high, (x - high.astype(F32)).astype(BF16)


def dot3(ah, al, bh, bl, dims=(((1,), (0,)), ((), ()))):
    d = functools.partial(lax.dot_general, dimension_numbers=dims, preferred_element_type=F32)
    return d(ah, bh) + (d(al, bh) + d(ah, bl))


def whole(ref, sem):
    return pltpu.make_async_copy(ref, ref, sem)


def kernel(
    g_hbm, w_hbm, rd_hbm, u_hbm, fh_hbm, fl_hbm, ih_hbm, il_hbm,
    sig_out, new_out,
    fh, fl, ih, il, gv, wv, pk, rv, ob, sg, above, below, ub, rd, ru, km, sf, es_h, es_l, el_h, el_l, total,
    load_sem, ret_sem, mat_sem, send_sem, xsend_sem, recv_sem, back_sem, sig_sem, hop_send, hop_recv,
):
    me = lax.axis_index("energy")
    k = lax.axis_index("cell")
    my_z = me // 4
    my_i = my_z // 2
    my_c = my_z % 2
    is_extra = jnp.equal(me % 4, my_i)
    has_up = k < 7
    has_down = k > 0

    def load_cell(c):
        for j, (source, target) in enumerate(((g_hbm, gv), (w_hbm, wv))):
            pltpu.make_async_copy(source.at[pl.ds(4 * c, 4)], target.at[pl.ds(4 * c, 4), pl.ds(0, 144)], load_sem.at[c, j]).start()

    load_cell(0)

    barrier = pltpu.get_barrier_semaphore()

    def greet(i, carry):
        pl.semaphore_signal(barrier, inc=1, device_id={"energy": lax.rem(me + i, PEERS)}, device_id_type=MESH)
        return carry

    lax.fori_loop(1, PEERS, greet, 0)

    @pl.when(has_up)
    def _():
        pl.semaphore_signal(barrier, inc=1, device_id={"cell": k + 1}, device_id_type=MESH)

    @pl.when(has_down)
    def _():
        pl.semaphore_signal(barrier, inc=1, device_id={"cell": k - 1}, device_id_type=MESH)

    load_cell(1)
    load_rd = pltpu.make_async_copy(rd_hbm, rd, ret_sem.at[0])
    load_ru = pltpu.make_async_copy(u_hbm, ru, ret_sem.at[1])
    load_mats = [
        pltpu.make_async_copy(source, target, mat_sem.at[i])
        for i, (source, target) in enumerate(((fh_hbm, fh), (fl_hbm, fl), (ih_hbm, ih), (il_hbm, il)))
    ]
    for copy in (*load_mats, load_rd, load_ru):
        copy.start()

    row = lax.broadcasted_iota(jnp.int32, (40, 128), 0)
    lane = lax.broadcasted_iota(jnp.int32, (40, 128), 1)
    slot_index = row * 128 + lane
    a_index = (slot_index * 43691) >> 22
    b_index = slot_index - a_index * B
    direct = b_index >= a_index
    diagonal = b_index == a_index
    near = lane >= 48

    def pack(c):
        for which, source in enumerate((gv, wv)):
            pltpu.make_async_copy(
                (g_hbm, w_hbm)[which].at[pl.ds(4 * c, 4)], source.at[pl.ds(4 * c, 4), pl.ds(0, 144)], load_sem.at[c, which]
            ).wait()

            for e in range(4):
                blk = 4 * c + e
                first, far = [], []
                for part in range(2):
                    first.append(source[blk, pl.ds(part, 40, stride=2), :])
                    here = source[blk, pl.ds(72 + part, 40, stride=2), :]
                    after = source[blk, pl.ds(74 + part, 40, stride=2), :]
                    far.append(pltpu.roll(jnp.where(near, here, after), 80, 1))
                re = jnp.where(direct, first[0], far[0])
                re = jnp.where(diagonal, far[1], re)
                im = jnp.where(direct, first[1], far[1])
                base = which * 8 + 2 * e
                pk[c, pl.ds(base, 40, stride=16), :] = re
                pk[c, pl.ds(base + 1, 40, stride=16), :] = im

    def outgoing(c, p):
        return pltpu.make_async_remote_copy(
            src_ref=pk.at[c, pl.ds(p * 16, 16)], dst_ref=rv.at[c, me], send_sem=send_sem.at[c], recv_sem=recv_sem.at[c],
            device_id={"energy": p}, device_id_type=MESH,
        )

    def extra_out(c, i):
        return pltpu.make_async_remote_copy(
            src_ref=pk.at[c, pl.ds((PEERS + i) * 16, 16)], dst_ref=rv.at[2, me], send_sem=xsend_sem.at[c, i],
            recv_sem=recv_sem.at[2], device_id={"energy": 4 * (2 * i + c) + i}, device_id_type=MESH,
        )

    def send(c):
        def start(i, carry):
            p = 2 * lax.rem(me // 2 + 16 + jnp.where(i % 2 == 1, (i % 16 + 1) // 2, -((i % 16) // 2)), 16) + i // 16

            @pl.when(p != me)
            def _():
                outgoing(c, p).start()

            return carry

        pltpu.make_async_copy(pk.at[c, pl.ds(me * 16, 16)], rv.at[c, me], recv_sem.at[c]).start()
        lax.fori_loop(0, PEERS, start, 0)

        for i in range(4):
            mine = jnp.equal(me, 4 * (2 * i + c) + i)

            @pl.when(jnp.logical_not(mine))
            def _(i=i):
                extra_out(c, i).start()

            @pl.when(mine)
            def _(i=i):
                pltpu.make_async_copy(pk.at[c, pl.ds((PEERS + i) * 16, 16)], rv.at[2, me], recv_sem.at[2]).start()


    pack(0)
    pl.semaphore_wait(barrier, 31 + has_up.astype(jnp.int32) + has_down.astype(jnp.int32))
    send(0)
    pack(1)
    send(1)

    def u_copy():
        return pltpu.make_async_remote_copy(
            src_ref=u_hbm.at[pl.ds(4, 4)], dst_ref=ub, send_sem=hop_send.at[0], recv_sem=hop_recv.at[0],
            device_id={"cell": k + 1}, device_id_type=MESH,
        )

    def down_copy():
        return pltpu.make_async_remote_copy(
            src_ref=sg.at[0], dst_ref=above, send_sem=hop_send.at[1], recv_sem=hop_recv.at[1],
            device_id={"cell": k - 1}, device_id_type=MESH,
        )

    def down_part(half):
        part = pl.ds(18 * half, 18)
        return pltpu.make_async_remote_copy(
            src_ref=sg.at[0, part], dst_ref=above.at[part], send_sem=hop_send.at[1], recv_sem=hop_recv.at[1],
            device_id={"cell": k - 1}, device_id_type=MESH,
        )

    def up_part(half):
        part = pl.ds(18 * half, 18)
        return pltpu.make_async_remote_copy(
            src_ref=sg.at[1, part], dst_ref=below.at[part], send_sem=hop_send.at[2], recv_sem=hop_recv.at[2],
            device_id={"cell": k + 1}, device_id_type=MESH,
        )

    def up_copy():
        return pltpu.make_async_remote_copy(
            src_ref=sg.at[1], dst_ref=below, send_sem=hop_send.at[2], recv_sem=hop_recv.at[2],
            device_id={"cell": k + 1}, device_id_type=MESH,
        )

    @pl.when(has_up)
    def _():
        u_copy().start()

    @pl.when(jnp.logical_not(has_up))
    def _():
        above[...] = jnp.zeros_like(above)

    @pl.when(jnp.logical_not(has_down))
    def _():
        below[...] = jnp.zeros_like(below)
        ub[...] = jnp.zeros_like(ub)

    def place(tile):
        return (tile % 2) * 18 + tile // 2

    def back(slot, c, tile, p):
        return pltpu.make_async_remote_copy(
            src_ref=ob.at[slot, p], dst_ref=sg.at[c, place(tile)], send_sem=back_sem.at[slot], recv_sem=sig_sem.at[c, tile % 2],
            device_id={"energy": p}, device_id_type=MESH,
        )

    def convolve(slot, c, tile):
        whole(rv.at[slot], recv_sem.at[slot]).wait()
        green = rv[slot, :, 0:8, :].reshape(256, 128)
        screen = rv[slot, :, 8:16, :].reshape(256, 128)
        xh, xl = split(jnp.concatenate([green, screen], 1))
        hat = dot3(fh[...], fl[...], xh, xl)
        xr, xi, yr, yi = (hat[128 * j:128 * j + 128] for j in range(4))
        xrg, xrw, xig, xiw = xr[:, :128], xr[:, 128:], xi[:, :128], xi[:, 128:]
        yrg, yrw, yig, yiw = yr[:, :128], yr[:, 128:], yi[:, :128], yi[:, 128:]
        xx_r = xrg * xrw - xig * xiw
        xx_i = xrg * xiw + xig * xrw
        yy_r = yrg * yrw - yig * yiw
        yy_i = yrg * yiw + yig * yrw
        xy_r = (xrg * yrw - xig * yiw) + (yrg * xrw - yig * xiw)
        xy_i = (xrg * yiw + xig * yrw) + (yrg * xiw + yig * xrw)
        main = jnp.concatenate([-xy_r, -xy_i, xx_r - yy_r, xx_i - yy_i], 0)
        diag = jnp.concatenate([-xx_r, -xx_i, -yy_r, -yy_i], 0)
        zh, zl = split(jnp.concatenate([main, diag], 1))
        out = dot3(ih[...], il[...], zh, zl)
        position = tile * 128 + lax.broadcasted_iota(jnp.int32, (256, 128), 1)
        on_diagonal = position == ((position * 43241) >> 22) * 97
        ob[slot] = jnp.where(on_diagonal, out[:, 128:], out[:, :128]).reshape(PEERS, 8, 128)

        pltpu.make_async_copy(ob.at[slot, me], sg.at[c, place(tile)], sig_sem.at[c, tile % 2]).start()

        def start(i, carry):
            back(slot, c, tile, lax.rem(me + i, PEERS)).start()
            return carry

        lax.fori_loop(1, PEERS, start, 0)

    row48 = lax.broadcasted_iota(jnp.int32, (48, 128), 0)
    lane48 = lax.broadcasted_iota(jnp.int32, (48, 128), 1)
    lane8 = lax.broadcasted_iota(jnp.int32, (8, 128), 1)
    lane24 = lax.broadcasted_iota(jnp.int32, (24, 128), 1)
    zero48 = jnp.zeros((80, 128), F32)
    zero32 = jnp.zeros((32, 128), F32)
    inside48 = lane48 < B

    def to_rows(u0, u1, u2, lane):
        r1 = jnp.where(lane < 32, pltpu.roll(u0, 32, 1), pltpu.roll(u1, 32, 1))
        r2 = jnp.where(lane < 64, pltpu.roll(u1, 64, 1), pltpu.roll(u2, 64, 1))
        return u0, r1, r2, pltpu.roll(u2, 96, 1)

    def to_tiles(r0, r1, r2, r3, lane):
        m1, m2, m3 = pltpu.roll(r1, 96, 1), pltpu.roll(r2, 64, 1), pltpu.roll(r3, 32, 1)
        return jnp.where(lane < 96, r0, m1), jnp.where(lane < 64, m1, m2), jnp.where(lane < 32, m2, m3)

    def store_pair(high, low, index, re, im):
        re = jnp.concatenate([re, zero32], 0)
        im = jnp.concatenate([im, zero32], 0)
        rh, rl = split(re)
        mh, ml = split(im)
        for ref, r, m in ((high, rh, mh), (low, rl, ml)):
            ref[index, 0:128, 0:128] = r
            ref[index, 0:128, 128:256] = m
            ref[index, 128:256, 0:128] = -m
            ref[index, 128:256, 128:256] = r

    def flat_store(matrices, out, blk):
        for part in range(2):
            tiles = to_tiles(*(matrices[blk, part, pl.ds(j, 24, stride=4), :] for j in range(4)), lane24)
            for j in range(3):
                out[blk, pl.ds(2 * j + part, 24, stride=6), :] = tiles[j]

    def unpack(index):
        base = 96 * index
        kr = km[base:base + 48, :]
        ki = km[base + 48:base + 96, :]
        krt = -jnp.concatenate([kr, zero48], 0).T
        kit = jnp.concatenate([ki, zero48], 0).T
        less, same = lane48 < row48, lane48 == row48
        top_r = jnp.where(less, krt[:48], jnp.where(same, 0.0, kr))
        top_i = jnp.where(less, kit[:48], ki)
        in_r = jnp.where(less, kr, jnp.where(same, 0.0, krt[:48]))
        in_i = jnp.where(less, ki, jnp.where(same, kr, kit[:48]))
        low_r = jnp.where(lane48 < 48, krt[48:96], pltpu.roll(in_r, 48, 1))
        low_i = jnp.where(lane48 < 48, kit[48:96], pltpu.roll(in_i, 48, 1))
        re = jnp.concatenate([jnp.where(inside48, top_r, 0.0), jnp.where(inside48, low_r, 0.0)], 0)
        im = jnp.concatenate([jnp.where(inside48, top_i, 0.0), jnp.where(inside48, low_i, 0.0)], 0)
        store_pair(es_h, es_l, index, re, im)
        if index < 8:
            sf[index, 0] = re
            sf[index, 1] = im

    def to_matrices(array):
        def take(t):
            t = place(t)
            return sg[array, t] if array < 2 else (above[t] if array == 2 else below[t])

        for q in range(12):
            for j, r in enumerate(to_rows(take(3 * q), take(3 * q + 1), take(3 * q + 2), lane8)):
                km[pl.ds(array * 384 + 4 * q + j, 8, stride=48), :] = r
        for index in range(4 * array, 4 * array + 4):
            unpack(index)

    lane96 = lax.broadcasted_iota(jnp.int32, (96, 128), 1)

    def matrix(source, blk, part):
        u = [source[blk, pl.ds(2 * j + part, 24, stride=6), :] for j in range(3)]
        for j, r in enumerate(to_rows(*u, lane24)):
            sf[blk, part, pl.ds(j, 24, stride=4), :] = r
        return jnp.where(lane96 < B, sf[blk, part], 0.0)

    def flip(x):
        return jnp.concatenate([x, zero32], 0).T[:96]

    def diag_prep(blk, carry):
        store_pair(el_h, el_l, blk, matrix(rd, blk, 0), matrix(rd, blk, 1))
        return carry

    def upper_prep(blk, carry):
        re, im = matrix(ru, blk, 0), matrix(ru, blk, 1)
        store_pair(el_h, el_l, 8 + blk, re, im)

        @pl.when(blk < 4)
        def _():
            store_pair(el_h, el_l, 20 + blk, flip(re), flip(im))

        return carry

    def below_prep(blk, carry):
        store_pair(el_h, el_l, 16 + blk, flip(matrix(ub, blk, 0)), flip(matrix(ub, blk, 1)))
        return carry

    transposed = (((1,), (1,)), ((), ()))

    def add_terms(middle, pairs):
        for e in range(4):
            left_h = jnp.concatenate([el_h[left + e, 0:96, :] for _, left, _ in pairs], 0)
            left_l = jnp.concatenate([el_l[left + e, 0:96, :] for _, left, _ in pairs], 0)
            xh, xl = split(dot3(left_h, left_l, es_h[middle + e], es_l[middle + e]))
            for i, (blk, left, first) in enumerate(pairs):
                rows = slice(96 * i, 96 * i + 96)
                value = dot3(xh[rows], xl[rows], el_h[left + e], el_l[left + e], transposed)
                for part in range(2):
                    half = value[:, 128 * part:128 * part + 128]
                    if first:
                        total[blk + e, part] = half
                    else:
                        total[blk + e, part] += half

    def finish(c):
        for blk in range(4 * c, 4 * c + 4):
            flat_store(total, new_out, blk)

    def sigma_flat():
        for blk in range(8):
            flat_store(sf, sig_out, blk)

    def convolve_cell(c):
        def step(j, inner):
            slot = jnp.where(j == 0, c, 2)
            tile = jnp.where(j == 0, me, PEERS + my_i)
            convolve(slot, c, tile)
            return inner

        lax.fori_loop(0, 1 + jnp.where(jnp.logical_and(is_extra, my_c == c), 1, 0), step, 0)

    load_rd.wait()
    lax.fori_loop(0, 8, diag_prep, 0)
    for copy in load_mats:
        copy.wait()
    convolve_cell(0)
    load_ru.wait()
    lax.fori_loop(0, 8, upper_prep, 0)
    convolve_cell(1)

    @pl.when(has_down)
    def _():
        u_copy().wait_recv()

    lax.fori_loop(0, 4, below_prep, 0)

    for half in range(2):
        whole(sg.at[0, pl.ds(18 * half, 18)], sig_sem.at[0, half]).wait()

        @pl.when(has_down)
        def _(half=half):
            down_part(half).start()

    to_matrices(0)
    add_terms(0, ((0, 0, True), (4, 20, True)))
    for half in range(2):
        whole(sg.at[1, pl.ds(18 * half, 18)], sig_sem.at[1, half]).wait()

        @pl.when(has_up)
        def _(half=half):
            up_part(half).start()

    to_matrices(1)
    add_terms(4, ((4, 4, False), (0, 8, False)))

    @pl.when(has_up)
    def _():
        down_copy().wait_recv()

    to_matrices(2)
    add_terms(8, ((4, 12, False),))
    finish(1)
    sigma_flat()

    @pl.when(has_down)
    def _():
        up_copy().wait_recv()

    to_matrices(3)
    add_terms(12, ((0, 16, False),))
    finish(0)

    for c in range(2):
        whole(pk.at[c, pl.ds(0, 31 * 16)], send_sem.at[c]).wait()
        for i in range(4):
            @pl.when(jnp.logical_not(jnp.equal(me, 4 * (2 * i + c) + i)))
            def _(c=c, i=i):
                extra_out(c, i).wait_send()
        whole(ob.at[c, pl.ds(0, 31)], back_sem.at[c]).wait()

    @pl.when(is_extra)
    def _():
        whole(ob.at[2, pl.ds(0, 31)], back_sem.at[2]).wait()

    @pl.when(has_up)
    def _():
        u_copy().wait_send()
        up_copy().wait_send()

    @pl.when(has_down)
    def _():
        down_copy().wait_send()


def publish_kernel(a, b, a_out, b_out, sems):
    copies = []
    for i, (src, dst) in enumerate(((a, a_out), (b, b_out))):
        for j in range(PIECES):
            part = pl.ds(j * (8 // PIECES), 8 // PIECES)
            copies.append(pltpu.make_async_copy(src.at[part], dst.at[part], sems.at[i, j]))
    for copy in copies:
        copy.start()
    for copy in copies:
        copy.wait()


def flat_view(x):
    return x.reshape(8, 2, 72, 128).transpose(0, 2, 1, 3).reshape(8, 144, 128)


def from_flat(y):
    return y.reshape(8, 72, 2, 128).transpose(0, 2, 1, 3).reshape(2, 4, 2, B * B)


def shards(glesser, wlesser, gret_diag, gret_upper):
    g, w, rd, ru = (flat_view(x) for x in (glesser, wlesser, gret_diag, gret_upper))
    forward, inverse = transforms()
    constants = [jnp.asarray(x) for x in (*two_terms(forward), *two_terms(inverse))]
    vmem = pl.BlockSpec(memory_space=pltpu.VMEM)
    hbm = pl.BlockSpec(memory_space=pl.ANY)
    dma = pltpu.SemaphoreType.DMA
    sigma, new = pl.pallas_call(
        kernel,
        out_shape=[pltpu.VMEM((8, 144, 128), F32)] * 2,
        in_specs=[hbm] * 8,
        out_specs=[vmem] * 2,
        scratch_shapes=[
            pltpu.VMEM((512, 256), BF16),
            pltpu.VMEM((512, 256), BF16),
            pltpu.VMEM((256, 512), BF16),
            pltpu.VMEM((256, 512), BF16),
            pltpu.VMEM((8, 160, 128), F32),
            pltpu.VMEM((8, 160, 128), F32),
            pltpu.VMEM((2, 640, 128), F32),
            pltpu.VMEM((3, PEERS, 16, 128), F32),
            pltpu.VMEM((3, PEERS, 8, 128), F32),
            pltpu.VMEM((2, HALF, 8, 128), F32),
            pltpu.VMEM((HALF, 8, 128), F32),
            pltpu.VMEM((HALF, 8, 128), F32),
            pltpu.VMEM((4, 144, 128), F32),
            pltpu.VMEM((8, 144, 128), F32),
            pltpu.VMEM((8, 144, 128), F32),
            pltpu.VMEM((4 * 384, 128), F32),
            pltpu.VMEM((8, 2, 96, 128), F32),
            pltpu.VMEM((16, 256, 256), BF16),
            pltpu.VMEM((16, 256, 256), BF16),
            pltpu.VMEM((24, 256, 256), BF16),
            pltpu.VMEM((24, 256, 256), BF16),
            pltpu.VMEM((8, 2, 96, 128), F32),
            dma((2, 2)), dma((2,)), dma((4,)), dma((2,)), dma((2, 4)), dma((3,)), dma((3,)), dma((2, 2)), dma((3,)), dma((3,)),
        ],
        compiler_params=pltpu.CompilerParams(collective_id=0, has_side_effects=True, vmem_limit_bytes=VMEM_LIMIT),
        name="update",
    )(g, w, rd, ru, *constants)
    sigma, new = pl.pallas_call(
        publish_kernel,
        out_shape=[jax.ShapeDtypeStruct((8, 144, 128), F32)] * 2,
        in_specs=[vmem] * 2,
        out_specs=[hbm] * 2,
        scratch_shapes=[dma((2, PIECES))],
        name="publish",
    )(*(pltpu.with_memory_space_constraint(x, pltpu.VMEM) for x in (sigma, new)))
    return from_flat(sigma), from_flat(new)


def solution(mesh):
    spec = P("cell", "energy", None, None)
    return jax.shard_map(shards, mesh=mesh, in_specs=(spec,) * 4, out_specs=(spec,) * 2, check_vma=False)
```

```python
import functools

import jax
import jax.numpy as jnp
import ml_dtypes
import numpy as np
from jax import lax
from jax.experimental import pallas as pl
from jax.experimental.pallas import tpu as pltpu
from jax.sharding import PartitionSpec as P

MESH = pl.DeviceIdType.MESH
B = 96
NE = 128
PEERS = 32
HALF = 36
F32 = jnp.float32
BF16 = jnp.bfloat16
PIECES = 4
VMEM_LIMIT = 56 * 1024 * 1024


def two_terms(x):
    high = x.astype(ml_dtypes.bfloat16)
    return high, (x - high.astype(np.float64)).astype(ml_dtypes.bfloat16)


def transforms():
    n = np.arange(NE)
    k = np.arange(NE)
    angle = 2.0 * np.pi / (4 * NE) * ((n[None, :] * (1 - 4 * k[:, None])) % (4 * NE))
    forward = np.zeros((2, 2, NE, NE, 2))
    scale = NE ** -0.5 / NE
    for part in range(2):
        forward[part, 0, :, :, part] = np.cos(angle)
        forward[part, 1, :, :, part] = np.sin(angle)
    inverse = np.concatenate([np.cos(angle).T, np.sin(angle).T], 1) * scale
    return forward.reshape(512, 256), inverse


def split(x):
    high = x.astype(BF16)
    return high, (x - high.astype(F32)).astype(BF16)


def dot3(ah, al, bh, bl, dims=(((1,), (0,)), ((), ()))):
    d = functools.partial(lax.dot_general, dimension_numbers=dims, preferred_element_type=F32)
    return d(ah, bh) + (d(al, bh) + d(ah, bl))


def whole(ref, sem):
    return pltpu.make_async_copy(ref, ref, sem)


def kernel(
    g_hbm, w_hbm, rd_hbm, u_hbm, fh_hbm, fl_hbm, ih_hbm, il_hbm,
    sig_out, new_out,
    fh, fl, ih, il, gv, wv, pk, rv, ob, sg, above, below, ub, rd, ru, km, sf, es_h, es_l, el_h, el_l, total,
    load_sem, ret_sem, mat_sem, send_sem, xsend_sem, recv_sem, back_sem, sig_sem, hop_send, hop_recv,
):
    me = lax.axis_index("energy")
    k = lax.axis_index("cell")
    my_z = me // 4
    my_i = my_z // 2
    my_c = my_z % 2
    is_extra = jnp.equal(me % 4, my_i)
    has_up = k < 7
    has_down = k > 0

    def load_cell(c):
        for j, (source, target) in enumerate(((g_hbm, gv), (w_hbm, wv))):
            pltpu.make_async_copy(source.at[pl.ds(4 * c, 4)], target.at[pl.ds(4 * c, 4), pl.ds(0, 144)], load_sem.at[c, j]).start()

    load_cell(0)

    barrier = pltpu.get_barrier_semaphore()

    def greet(i, carry):
        pl.semaphore_signal(barrier, inc=1, device_id={"energy": lax.rem(me + i, PEERS)}, device_id_type=MESH)
        return carry

    lax.fori_loop(1, PEERS, greet, 0)

    @pl.when(has_up)
    def _():
        pl.semaphore_signal(barrier, inc=1, device_id={"cell": k + 1}, device_id_type=MESH)

    @pl.when(has_down)
    def _():
        pl.semaphore_signal(barrier, inc=1, device_id={"cell": k - 1}, device_id_type=MESH)

    load_cell(1)
    load_rd = pltpu.make_async_copy(rd_hbm, rd, ret_sem.at[0])
    load_ru = pltpu.make_async_copy(u_hbm, ru, ret_sem.at[1])
    load_mats = [
        pltpu.make_async_copy(source, target, mat_sem.at[i])
        for i, (source, target) in enumerate(((fh_hbm, fh), (fl_hbm, fl), (ih_hbm, ih), (il_hbm, il)))
    ]
    for copy in (*load_mats, load_rd, load_ru):
        copy.start()

    row = lax.broadcasted_iota(jnp.int32, (40, 128), 0)
    lane = lax.broadcasted_iota(jnp.int32, (40, 128), 1)
    slot_index = row * 128 + lane
    a_index = (slot_index * 43691) >> 22
    b_index = slot_index - a_index * B
    direct = b_index >= a_index
    diagonal = b_index == a_index
    near = lane >= 48

    def pack(c):
        for which, source in enumerate((gv, wv)):
            pltpu.make_async_copy(
                (g_hbm, w_hbm)[which].at[pl.ds(4 * c, 4)], source.at[pl.ds(4 * c, 4), pl.ds(0, 144)], load_sem.at[c, which]
            ).wait()

            for e in range(4):
                blk = 4 * c + e
                first, far = [], []
                for part in range(2):
                    first.append(source[blk, pl.ds(part, 40, stride=2), :])
                    here = source[blk, pl.ds(72 + part, 40, stride=2), :]
                    after = source[blk, pl.ds(74 + part, 40, stride=2), :]
                    far.append(pltpu.roll(jnp.where(near, here, after), 80, 1))
                re = jnp.where(direct, first[0], far[0])
                re = jnp.where(diagonal, far[1], re)
                im = jnp.where(direct, first[1], far[1])
                base = which * 8 + 2 * e
                pk[c, pl.ds(base, 40, stride=16), :] = re
                pk[c, pl.ds(base + 1, 40, stride=16), :] = im

    def outgoing(c, p):
        return pltpu.make_async_remote_copy(
            src_ref=pk.at[c, pl.ds(p * 16, 16)], dst_ref=rv.at[c, me], send_sem=send_sem.at[c], recv_sem=recv_sem.at[c],
            device_id={"energy": p}, device_id_type=MESH,
        )

    def extra_out(c, i):
        return pltpu.make_async_remote_copy(
            src_ref=pk.at[c, pl.ds((PEERS + i) * 16, 16)], dst_ref=rv.at[2, me], send_sem=xsend_sem.at[c, i],
            recv_sem=recv_sem.at[2], device_id={"energy": 4 * (2 * i + c) + i}, device_id_type=MESH,
        )

    def send(c):
        def start(i, carry):
            p = 2 * lax.rem(me // 2 + 16 + jnp.where(i % 2 == 1, (i % 16 + 1) // 2, -((i % 16) // 2)), 16) + i // 16

            @pl.when(p != me)
            def _():
                outgoing(c, p).start()

            return carry

        pltpu.make_async_copy(pk.at[c, pl.ds(me * 16, 16)], rv.at[c, me], recv_sem.at[c]).start()
        lax.fori_loop(0, PEERS, start, 0)

        for i in range(4):
            mine = jnp.equal(me, 4 * (2 * i + c) + i)

            @pl.when(jnp.logical_not(mine))
            def _(i=i):
                extra_out(c, i).start()

            @pl.when(mine)
            def _(i=i):
                pltpu.make_async_copy(pk.at[c, pl.ds((PEERS + i) * 16, 16)], rv.at[2, me], recv_sem.at[2]).start()


    pack(0)
    pl.semaphore_wait(barrier, 31 + has_up.astype(jnp.int32) + has_down.astype(jnp.int32))
    send(0)
    pack(1)
    send(1)

    def u_copy():
        return pltpu.make_async_remote_copy(
            src_ref=u_hbm.at[pl.ds(4, 4)], dst_ref=ub, send_sem=hop_send.at[0], recv_sem=hop_recv.at[0],
            device_id={"cell": k + 1}, device_id_type=MESH,
        )

    def down_copy():
        return pltpu.make_async_remote_copy(
            src_ref=sg.at[0], dst_ref=above, send_sem=hop_send.at[1], recv_sem=hop_recv.at[1],
            device_id={"cell": k - 1}, device_id_type=MESH,
        )

    def down_part(half):
        part = pl.ds(18 * half, 18)
        return pltpu.make_async_remote_copy(
            src_ref=sg.at[0, part], dst_ref=above.at[part], send_sem=hop_send.at[1], recv_sem=hop_recv.at[1],
            device_id={"cell": k - 1}, device_id_type=MESH,
        )

    def up_part(half):
        part = pl.ds(18 * half, 18)
        return pltpu.make_async_remote_copy(
            src_ref=sg.at[1, part], dst_ref=below.at[part], send_sem=hop_send.at[2], recv_sem=hop_recv.at[2],
            device_id={"cell": k + 1}, device_id_type=MESH,
        )

    def up_copy():
        return pltpu.make_async_remote_copy(
            src_ref=sg.at[1], dst_ref=below, send_sem=hop_send.at[2], recv_sem=hop_recv.at[2],
            device_id={"cell": k + 1}, device_id_type=MESH,
        )

    @pl.when(has_up)
    def _():
        u_copy().start()

    @pl.when(jnp.logical_not(has_up))
    def _():
        above[...] = jnp.zeros_like(above)

    @pl.when(jnp.logical_not(has_down))
    def _():
        below[...] = jnp.zeros_like(below)
        ub[...] = jnp.zeros_like(ub)

    def place(tile):
        return (tile % 2) * 18 + tile // 2

    def back(slot, c, tile, p):
        return pltpu.make_async_remote_copy(
            src_ref=ob.at[slot, pl.ds(p * 8, 8)], dst_ref=sg.at[c, place(tile)], send_sem=back_sem.at[slot], recv_sem=sig_sem.at[c, tile % 2],
            device_id={"energy": p}, device_id_type=MESH,
        )

    def convolve(slot, c, tile):
        whole(rv.at[slot], recv_sem.at[slot]).wait()
        green = rv[slot, :, 0:8, :].reshape(256, 128)
        screen = rv[slot, :, 8:16, :].reshape(256, 128)
        xh, xl = split(jnp.concatenate([green, screen], 1))
        hat = dot3(fh[...], fl[...], xh, xl)
        xr, xi, yr, yi = (hat[128 * j:128 * j + 128] for j in range(4))
        xrg, xrw, xig, xiw = xr[:, :128], xr[:, 128:], xi[:, :128], xi[:, 128:]
        yrg, yrw, yig, yiw = yr[:, :128], yr[:, 128:], yi[:, :128], yi[:, 128:]
        xx_r = xrg * xrw - xig * xiw
        xx_i = xrg * xiw + xig * xrw
        yy_r = yrg * yrw - yig * yiw
        yy_i = yrg * yiw + yig * yrw
        xy_r = (xrg * yrw - xig * yiw) + (yrg * xrw - yig * xiw)
        xy_i = (xrg * yiw + xig * yrw) + (yrg * xiw + yig * xrw)
        products = jnp.concatenate([jnp.concatenate(z, 0) for z in ((xx_r, xx_i), (yy_r, yy_i), (xy_r, xy_i))], 1)
        zh, zl = split(products)
        out = dot3(ih[...], il[...], zh, zl)
        xx, yy, xy = (out[:, 128 * j:128 * j + 128] for j in range(3))
        position = tile * 128 + lax.broadcasted_iota(jnp.int32, (128, 128), 1)
        on_diagonal = position == ((position * 43241) >> 22) * 97
        ob[slot, pl.ds(0, 128, stride=2), :] = -jnp.where(on_diagonal, xx, xy)
        ob[slot, pl.ds(1, 128, stride=2), :] = jnp.where(on_diagonal, 0.0, xx) - yy

        pltpu.make_async_copy(ob.at[slot, pl.ds(me * 8, 8)], sg.at[c, place(tile)], sig_sem.at[c, tile % 2]).start()

        def start(i, carry):
            back(slot, c, tile, lax.rem(me + PEERS + jnp.where(i % 2 == 1, 16 - i // 2, i // 2 - 16), PEERS)).start()
            return carry

        lax.fori_loop(1, PEERS, start, 0)

    row48 = lax.broadcasted_iota(jnp.int32, (48, 128), 0)
    lane48 = lax.broadcasted_iota(jnp.int32, (48, 128), 1)
    lane8 = lax.broadcasted_iota(jnp.int32, (8, 128), 1)
    lane24 = lax.broadcasted_iota(jnp.int32, (24, 128), 1)
    zero48 = jnp.zeros((80, 128), F32)
    zero32 = jnp.zeros((32, 128), F32)
    inside48 = lane48 < B

    def to_rows(u0, u1, u2, lane):
        r1 = jnp.where(lane < 32, pltpu.roll(u0, 32, 1), pltpu.roll(u1, 32, 1))
        r2 = jnp.where(lane < 64, pltpu.roll(u1, 64, 1), pltpu.roll(u2, 64, 1))
        return u0, r1, r2, pltpu.roll(u2, 96, 1)

    def to_tiles(r0, r1, r2, r3, lane):
        m1, m2, m3 = pltpu.roll(r1, 96, 1), pltpu.roll(r2, 64, 1), pltpu.roll(r3, 32, 1)
        return jnp.where(lane < 96, r0, m1), jnp.where(lane < 64, m1, m2), jnp.where(lane < 32, m2, m3)

    def store_pair(high, low, index, re, im):
        re = jnp.concatenate([re, zero32], 0)
        im = jnp.concatenate([im, zero32], 0)
        rh, rl = split(re)
        mh, ml = split(im)
        for ref, r, m in ((high, rh, mh), (low, rl, ml)):
            ref[index, 0:128, 0:128] = r
            ref[index, 0:128, 128:256] = m
            ref[index, 128:256, 0:128] = -m
            ref[index, 128:256, 128:256] = r

    def flat_store(matrices, out, blk):
        for part in range(2):
            tiles = to_tiles(*(matrices[blk, part, pl.ds(j, 24, stride=4), :] for j in range(4)), lane24)
            for j in range(3):
                out[blk, pl.ds(2 * j + part, 24, stride=6), :] = tiles[j]

    def unpack(index):
        base = 96 * index
        kr = km[base:base + 48, :]
        ki = km[base + 48:base + 96, :]
        krt = -jnp.concatenate([kr, zero48], 0).T
        kit = jnp.concatenate([ki, zero48], 0).T
        less, same = lane48 < row48, lane48 == row48
        top_r = jnp.where(less, krt[:48], jnp.where(same, 0.0, kr))
        top_i = jnp.where(less, kit[:48], ki)
        in_r = jnp.where(less, kr, jnp.where(same, 0.0, krt[:48]))
        in_i = jnp.where(less, ki, jnp.where(same, kr, kit[:48]))
        low_r = jnp.where(lane48 < 48, krt[48:96], pltpu.roll(in_r, 48, 1))
        low_i = jnp.where(lane48 < 48, kit[48:96], pltpu.roll(in_i, 48, 1))
        re = jnp.concatenate([jnp.where(inside48, top_r, 0.0), jnp.where(inside48, low_r, 0.0)], 0)
        im = jnp.concatenate([jnp.where(inside48, top_i, 0.0), jnp.where(inside48, low_i, 0.0)], 0)
        store_pair(es_h, es_l, index, re, im)
        if index < 8:
            sf[index, 0] = re
            sf[index, 1] = im

    def to_matrices(array):
        def take(t):
            t = place(t)
            return sg[array, t] if array < 2 else (above[t] if array == 2 else below[t])

        for q in range(12):
            for j, r in enumerate(to_rows(take(3 * q), take(3 * q + 1), take(3 * q + 2), lane8)):
                km[pl.ds(array * 384 + 4 * q + j, 8, stride=48), :] = r
        for index in range(4 * array, 4 * array + 4):
            unpack(index)

    lane96 = lax.broadcasted_iota(jnp.int32, (96, 128), 1)

    def matrix(source, blk, part):
        u = [source[blk, pl.ds(2 * j + part, 24, stride=6), :] for j in range(3)]
        for j, r in enumerate(to_rows(*u, lane24)):
            sf[blk, part, pl.ds(j, 24, stride=4), :] = r
        return jnp.where(lane96 < B, sf[blk, part], 0.0)

    def flip(x):
        return jnp.concatenate([x, zero32], 0).T[:96]

    def diag_prep(blk, carry):
        store_pair(el_h, el_l, blk, matrix(rd, blk, 0), matrix(rd, blk, 1))
        return carry

    def upper_prep(blk, carry):
        re, im = matrix(ru, blk, 0), matrix(ru, blk, 1)
        store_pair(el_h, el_l, 8 + blk, re, im)

        @pl.when(blk < 4)
        def _():
            store_pair(el_h, el_l, 20 + blk, flip(re), flip(im))

        return carry

    def below_prep(blk, carry):
        store_pair(el_h, el_l, 16 + blk, flip(matrix(ub, blk, 0)), flip(matrix(ub, blk, 1)))
        return carry

    transposed = (((1,), (1,)), ((), ()))

    def add_terms(middle, pairs):
        for e in range(4):
            left_h = jnp.concatenate([el_h[left + e, 0:96, :] for _, left, _ in pairs], 0)
            left_l = jnp.concatenate([el_l[left + e, 0:96, :] for _, left, _ in pairs], 0)
            xh, xl = split(dot3(left_h, left_l, es_h[middle + e], es_l[middle + e]))
            for i, (blk, left, first) in enumerate(pairs):
                rows = slice(96 * i, 96 * i + 96)
                value = dot3(xh[rows], xl[rows], el_h[left + e], el_l[left + e], transposed)
                for part in range(2):
                    half = value[:, 128 * part:128 * part + 128]
                    if first:
                        total[blk + e, part] = half
                    else:
                        total[blk + e, part] += half

    def finish(c):
        for blk in range(4 * c, 4 * c + 4):
            flat_store(total, new_out, blk)

    def sigma_flat():
        for blk in range(8):
            flat_store(sf, sig_out, blk)

    def convolve_cell(c):
        def step(j, inner):
            slot = jnp.where(j == 0, c, 2)
            tile = jnp.where(j == 0, me, PEERS + my_i)
            convolve(slot, c, tile)
            return inner

        lax.fori_loop(0, 1 + jnp.where(jnp.logical_and(is_extra, my_c == c), 1, 0), step, 0)

    load_rd.wait()
    lax.fori_loop(0, 8, diag_prep, 0)
    for copy in load_mats:
        copy.wait()
    convolve_cell(0)
    load_ru.wait()
    lax.fori_loop(0, 8, upper_prep, 0)
    convolve_cell(1)

    @pl.when(has_down)
    def _():
        u_copy().wait_recv()

    lax.fori_loop(0, 4, below_prep, 0)

    for half in range(2):
        whole(sg.at[0, pl.ds(18 * half, 18)], sig_sem.at[0, half]).wait()

        @pl.when(has_down)
        def _(half=half):
            down_part(half).start()

    to_matrices(0)
    add_terms(0, ((0, 0, True), (4, 20, True)))
    for half in range(2):
        whole(sg.at[1, pl.ds(18 * half, 18)], sig_sem.at[1, half]).wait()

        @pl.when(has_up)
        def _(half=half):
            up_part(half).start()

    to_matrices(1)
    add_terms(4, ((4, 4, False), (0, 8, False)))

    @pl.when(has_up)
    def _():
        down_copy().wait_recv()

    to_matrices(2)
    add_terms(8, ((4, 12, False),))
    finish(1)
    sigma_flat()

    for c in range(2):
        whole(pk.at[c, pl.ds(0, 31 * 16)], send_sem.at[c]).wait()
        for i in range(4):
            @pl.when(jnp.logical_not(jnp.equal(me, 4 * (2 * i + c) + i)))
            def _(c=c, i=i):
                extra_out(c, i).wait_send()
        whole(ob.at[c, pl.ds(0, 31 * 8)], back_sem.at[c]).wait()

    @pl.when(is_extra)
    def _():
        whole(ob.at[2, pl.ds(0, 31 * 8)], back_sem.at[2]).wait()

    @pl.when(has_up)
    def _():
        u_copy().wait_send()

    @pl.when(has_down)
    def _():
        down_copy().wait_send()

    @pl.when(has_down)
    def _():
        up_copy().wait_recv()

    to_matrices(3)
    add_terms(12, ((0, 16, False),))
    finish(0)

    @pl.when(has_up)
    def _():
        up_copy().wait_send()


def publish_kernel(a, b, a_out, b_out, sems):
    copies = []
    for i, (src, dst) in enumerate(((a, a_out), (b, b_out))):
        for j in range(PIECES):
            part = pl.ds(j * (8 // PIECES), 8 // PIECES)
            copies.append(pltpu.make_async_copy(src.at[part], dst.at[part], sems.at[i, j]))
    for copy in copies:
        copy.start()
    for copy in copies:
        copy.wait()


def flat_view(x):
    return x.reshape(8, 2, 72, 128).transpose(0, 2, 1, 3).reshape(8, 144, 128)


def from_flat(y):
    return y.reshape(8, 72, 2, 128).transpose(0, 2, 1, 3).reshape(2, 4, 2, B * B)


def shards(glesser, wlesser, gret_diag, gret_upper):
    g, w, rd, ru = (flat_view(x) for x in (glesser, wlesser, gret_diag, gret_upper))
    forward, inverse = transforms()
    constants = [jnp.asarray(x) for x in (*two_terms(forward), *two_terms(inverse))]
    vmem = pl.BlockSpec(memory_space=pltpu.VMEM)
    hbm = pl.BlockSpec(memory_space=pl.ANY)
    dma = pltpu.SemaphoreType.DMA
    sigma, new = pl.pallas_call(
        kernel,
        out_shape=[pltpu.VMEM((8, 144, 128), F32)] * 2,
        in_specs=[hbm] * 8,
        out_specs=[vmem] * 2,
        scratch_shapes=[
            pltpu.VMEM((512, 256), BF16),
            pltpu.VMEM((512, 256), BF16),
            pltpu.VMEM((128, 256), BF16),
            pltpu.VMEM((128, 256), BF16),
            pltpu.VMEM((8, 160, 128), F32),
            pltpu.VMEM((8, 160, 128), F32),
            pltpu.VMEM((2, 640, 128), F32),
            pltpu.VMEM((3, PEERS, 16, 128), F32),
            pltpu.VMEM((3, PEERS * 8, 128), F32),
            pltpu.VMEM((2, HALF, 8, 128), F32),
            pltpu.VMEM((HALF, 8, 128), F32),
            pltpu.VMEM((HALF, 8, 128), F32),
            pltpu.VMEM((4, 144, 128), F32),
            pltpu.VMEM((8, 144, 128), F32),
            pltpu.VMEM((8, 144, 128), F32),
            pltpu.VMEM((4 * 384, 128), F32),
            pltpu.VMEM((8, 2, 96, 128), F32),
            pltpu.VMEM((16, 256, 256), BF16),
            pltpu.VMEM((16, 256, 256), BF16),
            pltpu.VMEM((24, 256, 256), BF16),
            pltpu.VMEM((24, 256, 256), BF16),
            pltpu.VMEM((8, 2, 96, 128), F32),
            dma((2, 2)), dma((2,)), dma((4,)), dma((2,)), dma((2, 4)), dma((3,)), dma((3,)), dma((2, 2)), dma((3,)), dma((3,)),
        ],
        compiler_params=pltpu.CompilerParams(collective_id=0, has_side_effects=True, vmem_limit_bytes=VMEM_LIMIT),
        name="update",
    )(g, w, rd, ru, *constants)
    sigma, new = pl.pallas_call(
        publish_kernel,
        out_shape=[jax.ShapeDtypeStruct((8, 144, 128), F32)] * 2,
        in_specs=[vmem] * 2,
        out_specs=[hbm] * 2,
        scratch_shapes=[dma((2, PIECES))],
        name="publish",
    )(*(pltpu.with_memory_space_constraint(x, pltpu.VMEM) for x in (sigma, new)))
    return from_flat(sigma), from_flat(new)


def solution(mesh):
    spec = P("cell", "energy", None, None)
    return jax.shard_map(shards, mesh=mesh, in_specs=(spec,) * 4, out_specs=(spec,) * 2, check_vma=False)
```

```python
import functools

import jax
import jax.numpy as jnp
import ml_dtypes
import numpy as np
from jax import lax
from jax.experimental import pallas as pl
from jax.experimental.pallas import tpu as pltpu
from jax.sharding import PartitionSpec as P

MESH = pl.DeviceIdType.MESH
B = 96
NE = 128
PEERS = 32
HALF = 36
F32 = jnp.float32
BF16 = jnp.bfloat16
PIECES = 4
VMEM_LIMIT = 56 * 1024 * 1024


def two_terms(x):
    high = x.astype(ml_dtypes.bfloat16)
    return high, (x - high.astype(np.float64)).astype(ml_dtypes.bfloat16)


def transforms():
    n = np.arange(NE)
    k = np.arange(NE)
    angle = 2.0 * np.pi / (4 * NE) * ((n[None, :] * (1 - 4 * k[:, None])) % (4 * NE))
    forward = np.zeros((2, 2, NE, NE, 2))
    scale = NE ** -0.5 / NE
    for part in range(2):
        forward[part, 0, :, :, part] = np.cos(angle)
        forward[part, 1, :, :, part] = np.sin(angle)
    inverse = np.concatenate([np.cos(angle).T, np.sin(angle).T], 1) * scale
    return forward.reshape(512, 256), inverse


def split(x):
    high = x.astype(BF16)
    return high, (x - high.astype(F32)).astype(BF16)


def dot3(ah, al, bh, bl, dims=(((1,), (0,)), ((), ()))):
    d = functools.partial(lax.dot_general, dimension_numbers=dims, preferred_element_type=F32)
    return d(ah, bh) + (d(al, bh) + d(ah, bl))


def whole(ref, sem):
    return pltpu.make_async_copy(ref, ref, sem)


def kernel(
    g_hbm, w_hbm, rd_hbm, u_hbm, fh_hbm, fl_hbm, ih_hbm, il_hbm,
    sig_out, new_out,
    fh, fl, ih, il, gv, wv, pk, rv, ob, sg, above, below, ub, rd, ru, km, sf, es_h, es_l, el_h, el_l, total,
    load_sem, ret_sem, mat_sem, send_sem, xsend_sem, recv_sem, back_sem, sig_sem, hop_send, hop_recv,
):
    me = lax.axis_index("energy")
    k = lax.axis_index("cell")
    my_z = me // 4
    my_i = my_z // 2
    my_c = my_z % 2
    is_extra = jnp.equal(me % 4, my_i)
    has_up = k < 7
    has_down = k > 0

    def load_cell(c):
        for j, (source, target) in enumerate(((g_hbm, gv), (w_hbm, wv))):
            pltpu.make_async_copy(source.at[pl.ds(4 * c, 4)], target.at[pl.ds(4 * c, 4), pl.ds(0, 144)], load_sem.at[c, j]).start()

    load_cell(0)

    barrier = pltpu.get_barrier_semaphore()

    def greet(i, carry):
        pl.semaphore_signal(barrier, inc=1, device_id={"energy": lax.rem(me + i, PEERS)}, device_id_type=MESH)
        return carry

    lax.fori_loop(1, PEERS, greet, 0)

    @pl.when(has_up)
    def _():
        pl.semaphore_signal(barrier, inc=1, device_id={"cell": k + 1}, device_id_type=MESH)

    @pl.when(has_down)
    def _():
        pl.semaphore_signal(barrier, inc=1, device_id={"cell": k - 1}, device_id_type=MESH)

    load_cell(1)
    load_rd = pltpu.make_async_copy(rd_hbm, rd, ret_sem.at[0])
    load_ru = pltpu.make_async_copy(u_hbm, ru, ret_sem.at[1])
    load_mats = [
        pltpu.make_async_copy(source, target, mat_sem.at[i])
        for i, (source, target) in enumerate(((fh_hbm, fh), (fl_hbm, fl), (ih_hbm, ih), (il_hbm, il)))
    ]
    for copy in (*load_mats, load_rd, load_ru):
        copy.start()

    row = lax.broadcasted_iota(jnp.int32, (40, 128), 0)
    lane = lax.broadcasted_iota(jnp.int32, (40, 128), 1)
    slot_index = row * 128 + lane
    a_index = (slot_index * 43691) >> 22
    b_index = slot_index - a_index * B
    direct = b_index >= a_index
    diagonal = b_index == a_index
    near = lane >= 48

    def pack(c):
        for which, source in enumerate((gv, wv)):
            pltpu.make_async_copy(
                (g_hbm, w_hbm)[which].at[pl.ds(4 * c, 4)], source.at[pl.ds(4 * c, 4), pl.ds(0, 144)], load_sem.at[c, which]
            ).wait()

            for e in range(4):
                blk = 4 * c + e
                first, far = [], []
                for part in range(2):
                    first.append(source[blk, pl.ds(part, 40, stride=2), :])
                    here = source[blk, pl.ds(72 + part, 40, stride=2), :]
                    after = source[blk, pl.ds(74 + part, 40, stride=2), :]
                    far.append(pltpu.roll(jnp.where(near, here, after), 80, 1))
                re = jnp.where(direct, first[0], far[0])
                re = jnp.where(diagonal, far[1], re)
                im = jnp.where(direct, first[1], far[1])
                base = which * 8 + 2 * e
                pk[c, pl.ds(base, 40, stride=16), :] = re
                pk[c, pl.ds(base + 1, 40, stride=16), :] = im

    def outgoing(c, p):
        return pltpu.make_async_remote_copy(
            src_ref=pk.at[c, pl.ds(p * 16, 16)], dst_ref=rv.at[c, me], send_sem=send_sem.at[c], recv_sem=recv_sem.at[c],
            device_id={"energy": p}, device_id_type=MESH,
        )

    def extra_out(c, i):
        return pltpu.make_async_remote_copy(
            src_ref=pk.at[c, pl.ds((PEERS + i) * 16, 16)], dst_ref=rv.at[2, me], send_sem=xsend_sem.at[c, i],
            recv_sem=recv_sem.at[2], device_id={"energy": 4 * (2 * i + c) + i}, device_id_type=MESH,
        )

    def send(c):
        def start(i, carry):
            p = 4 * lax.rem(me // 4 + 8 + jnp.where(i % 2 == 1, (i % 8 + 1) // 2, -((i % 8) // 2)), 8) + lax.rem(4 - i // 8, 4)

            @pl.when(p != me)
            def _():
                outgoing(c, p).start()

            return carry

        pltpu.make_async_copy(pk.at[c, pl.ds(me * 16, 16)], rv.at[c, me], recv_sem.at[c]).start()
        lax.fori_loop(0, PEERS, start, 0)

        for i in range(4):
            mine = jnp.equal(me, 4 * (2 * i + c) + i)

            @pl.when(jnp.logical_not(mine))
            def _(i=i):
                extra_out(c, i).start()

            @pl.when(mine)
            def _(i=i):
                pltpu.make_async_copy(pk.at[c, pl.ds((PEERS + i) * 16, 16)], rv.at[2, me], recv_sem.at[2]).start()


    pack(0)
    pl.semaphore_wait(barrier, 31 + has_up.astype(jnp.int32) + has_down.astype(jnp.int32))
    send(0)
    pack(1)
    send(1)

    def u_copy():
        return pltpu.make_async_remote_copy(
            src_ref=u_hbm.at[pl.ds(4, 4)], dst_ref=ub, send_sem=hop_send.at[0], recv_sem=hop_recv.at[0],
            device_id={"cell": k + 1}, device_id_type=MESH,
        )

    def down_copy():
        return pltpu.make_async_remote_copy(
            src_ref=sg.at[0], dst_ref=above, send_sem=hop_send.at[1], recv_sem=hop_recv.at[1],
            device_id={"cell": k - 1}, device_id_type=MESH,
        )

    def down_part(half):
        part = pl.ds(18 * half, 18)
        return pltpu.make_async_remote_copy(
            src_ref=sg.at[0, part], dst_ref=above.at[part], send_sem=hop_send.at[1], recv_sem=hop_recv.at[1],
            device_id={"cell": k - 1}, device_id_type=MESH,
        )

    def up_part(half):
        part = pl.ds(18 * half, 18)
        return pltpu.make_async_remote_copy(
            src_ref=sg.at[1, part], dst_ref=below.at[part], send_sem=hop_send.at[2], recv_sem=hop_recv.at[2],
            device_id={"cell": k + 1}, device_id_type=MESH,
        )

    def up_copy():
        return pltpu.make_async_remote_copy(
            src_ref=sg.at[1], dst_ref=below, send_sem=hop_send.at[2], recv_sem=hop_recv.at[2],
            device_id={"cell": k + 1}, device_id_type=MESH,
        )

    @pl.when(has_up)
    def _():
        u_copy().start()

    @pl.when(jnp.logical_not(has_up))
    def _():
        above[...] = jnp.zeros_like(above)

    @pl.when(jnp.logical_not(has_down))
    def _():
        below[...] = jnp.zeros_like(below)
        ub[...] = jnp.zeros_like(ub)

    def place(tile):
        return (tile % 2) * 18 + tile // 2

    def back(slot, c, tile, p):
        return pltpu.make_async_remote_copy(
            src_ref=ob.at[slot, pl.ds(p * 8, 8)], dst_ref=sg.at[c, place(tile)], send_sem=back_sem.at[slot], recv_sem=sig_sem.at[c, tile % 2],
            device_id={"energy": p}, device_id_type=MESH,
        )

    def convolve(slot, c, tile):
        whole(rv.at[slot], recv_sem.at[slot]).wait()
        green = rv[slot, :, 0:8, :].reshape(256, 128)
        screen = rv[slot, :, 8:16, :].reshape(256, 128)
        xh, xl = split(jnp.concatenate([green, screen], 1))
        hat = dot3(fh[...], fl[...], xh, xl)
        xr, xi, yr, yi = (hat[128 * j:128 * j + 128] for j in range(4))
        xrg, xrw, xig, xiw = xr[:, :128], xr[:, 128:], xi[:, :128], xi[:, 128:]
        yrg, yrw, yig, yiw = yr[:, :128], yr[:, 128:], yi[:, :128], yi[:, 128:]
        xx_r = xrg * xrw - xig * xiw
        xx_i = xrg * xiw + xig * xrw
        yy_r = yrg * yrw - yig * yiw
        yy_i = yrg * yiw + yig * yrw
        xy_r = (xrg * yrw - xig * yiw) + (yrg * xrw - yig * xiw)
        xy_i = (xrg * yiw + xig * yrw) + (yrg * xiw + yig * xrw)
        products = jnp.concatenate([jnp.concatenate(z, 0) for z in ((xx_r, xx_i), (yy_r, yy_i), (xy_r, xy_i))], 1)
        zh, zl = split(products)
        out = dot3(ih[...], il[...], zh, zl)
        xx, yy, xy = (out[:, 128 * j:128 * j + 128] for j in range(3))
        position = tile * 128 + lax.broadcasted_iota(jnp.int32, (128, 128), 1)
        on_diagonal = position == ((position * 43241) >> 22) * 97
        ob[slot, pl.ds(0, 128, stride=2), :] = -jnp.where(on_diagonal, xx, xy)
        ob[slot, pl.ds(1, 128, stride=2), :] = jnp.where(on_diagonal, 0.0, xx) - yy

        pltpu.make_async_copy(ob.at[slot, pl.ds(me * 8, 8)], sg.at[c, place(tile)], sig_sem.at[c, tile % 2]).start()

        def start(i, carry):
            back(slot, c, tile, lax.rem(me + PEERS + jnp.where(i % 2 == 1, 16 - i // 2, i // 2 - 16), PEERS)).start()
            return carry

        lax.fori_loop(1, PEERS, start, 0)

    row48 = lax.broadcasted_iota(jnp.int32, (48, 128), 0)
    lane48 = lax.broadcasted_iota(jnp.int32, (48, 128), 1)
    lane8 = lax.broadcasted_iota(jnp.int32, (8, 128), 1)
    lane24 = lax.broadcasted_iota(jnp.int32, (24, 128), 1)
    zero48 = jnp.zeros((80, 128), F32)
    zero32 = jnp.zeros((32, 128), F32)
    inside48 = lane48 < B

    def to_rows(u0, u1, u2, lane):
        r1 = jnp.where(lane < 32, pltpu.roll(u0, 32, 1), pltpu.roll(u1, 32, 1))
        r2 = jnp.where(lane < 64, pltpu.roll(u1, 64, 1), pltpu.roll(u2, 64, 1))
        return u0, r1, r2, pltpu.roll(u2, 96, 1)

    def to_tiles(r0, r1, r2, r3, lane):
        m1, m2, m3 = pltpu.roll(r1, 96, 1), pltpu.roll(r2, 64, 1), pltpu.roll(r3, 32, 1)
        return jnp.where(lane < 96, r0, m1), jnp.where(lane < 64, m1, m2), jnp.where(lane < 32, m2, m3)

    def store_pair(high, low, index, re, im):
        re = jnp.concatenate([re, zero32], 0)
        im = jnp.concatenate([im, zero32], 0)
        rh, rl = split(re)
        mh, ml = split(im)
        for ref, r, m in ((high, rh, mh), (low, rl, ml)):
            ref[index, 0:128, 0:128] = r
            ref[index, 0:128, 128:256] = m
            ref[index, 128:256, 0:128] = -m
            ref[index, 128:256, 128:256] = r

    def flat_store(matrices, out, blk):
        for part in range(2):
            tiles = to_tiles(*(matrices[blk, part, pl.ds(j, 24, stride=4), :] for j in range(4)), lane24)
            for j in range(3):
                out[blk, pl.ds(2 * j + part, 24, stride=6), :] = tiles[j]

    def unpack(index):
        base = 96 * index
        kr = km[base:base + 48, :]
        ki = km[base + 48:base + 96, :]
        krt = -jnp.concatenate([kr, zero48], 0).T
        kit = jnp.concatenate([ki, zero48], 0).T
        less, same = lane48 < row48, lane48 == row48
        top_r = jnp.where(less, krt[:48], jnp.where(same, 0.0, kr))
        top_i = jnp.where(less, kit[:48], ki)
        in_r = jnp.where(less, kr, jnp.where(same, 0.0, krt[:48]))
        in_i = jnp.where(less, ki, jnp.where(same, kr, kit[:48]))
        low_r = jnp.where(lane48 < 48, krt[48:96], pltpu.roll(in_r, 48, 1))
        low_i = jnp.where(lane48 < 48, kit[48:96], pltpu.roll(in_i, 48, 1))
        re = jnp.concatenate([jnp.where(inside48, top_r, 0.0), jnp.where(inside48, low_r, 0.0)], 0)
        im = jnp.concatenate([jnp.where(inside48, top_i, 0.0), jnp.where(inside48, low_i, 0.0)], 0)
        store_pair(es_h, es_l, index, re, im)
        if index < 8:
            sf[index, 0] = re
            sf[index, 1] = im

    def to_matrices(array):
        def take(t):
            t = place(t)
            return sg[array, t] if array < 2 else (above[t] if array == 2 else below[t])

        for q in range(12):
            for j, r in enumerate(to_rows(take(3 * q), take(3 * q + 1), take(3 * q + 2), lane8)):
                km[pl.ds(array * 384 + 4 * q + j, 8, stride=48), :] = r
        for index in range(4 * array, 4 * array + 4):
            unpack(index)

    lane96 = lax.broadcasted_iota(jnp.int32, (96, 128), 1)

    def matrix(source, blk, part):
        u = [source[blk, pl.ds(2 * j + part, 24, stride=6), :] for j in range(3)]
        for j, r in enumerate(to_rows(*u, lane24)):
            sf[blk, part, pl.ds(j, 24, stride=4), :] = r
        return jnp.where(lane96 < B, sf[blk, part], 0.0)

    def flip(x):
        return jnp.concatenate([x, zero32], 0).T[:96]

    def diag_prep(blk, carry):
        store_pair(el_h, el_l, blk, matrix(rd, blk, 0), matrix(rd, blk, 1))
        return carry

    def upper_prep(blk, carry):
        re, im = matrix(ru, blk, 0), matrix(ru, blk, 1)
        store_pair(el_h, el_l, 8 + blk, re, im)

        @pl.when(blk < 4)
        def _():
            store_pair(el_h, el_l, 20 + blk, flip(re), flip(im))

        return carry

    def below_prep(blk, carry):
        store_pair(el_h, el_l, 16 + blk, flip(matrix(ub, blk, 0)), flip(matrix(ub, blk, 1)))
        return carry

    transposed = (((1,), (1,)), ((), ()))

    def add_terms(middle, pairs):
        for e in range(4):
            left_h = jnp.concatenate([el_h[left + e, 0:96, :] for _, left, _ in pairs], 0)
            left_l = jnp.concatenate([el_l[left + e, 0:96, :] for _, left, _ in pairs], 0)
            xh, xl = split(dot3(left_h, left_l, es_h[middle + e], es_l[middle + e]))
            for i, (blk, left, first) in enumerate(pairs):
                rows = slice(96 * i, 96 * i + 96)
                value = dot3(xh[rows], xl[rows], el_h[left + e], el_l[left + e], transposed)
                for part in range(2):
                    half = value[:, 128 * part:128 * part + 128]
                    if first:
                        total[blk + e, part] = half
                    else:
                        total[blk + e, part] += half

    def finish(c):
        for blk in range(4 * c, 4 * c + 4):
            flat_store(total, new_out, blk)

    def sigma_flat():
        for blk in range(8):
            flat_store(sf, sig_out, blk)

    def convolve_cell(c):
        def step(j, inner):
            slot = jnp.where(j == 0, c, 2)
            tile = jnp.where(j == 0, me, PEERS + my_i)
            convolve(slot, c, tile)
            return inner

        lax.fori_loop(0, 1 + jnp.where(jnp.logical_and(is_extra, my_c == c), 1, 0), step, 0)

    load_rd.wait()
    lax.fori_loop(0, 8, diag_prep, 0)
    for copy in load_mats:
        copy.wait()
    convolve_cell(0)
    load_ru.wait()
    lax.fori_loop(0, 8, upper_prep, 0)
    convolve_cell(1)

    @pl.when(has_down)
    def _():
        u_copy().wait_recv()

    lax.fori_loop(0, 4, below_prep, 0)

    for half in range(2):
        whole(sg.at[0, pl.ds(18 * half, 18)], sig_sem.at[0, half]).wait()

        @pl.when(has_down)
        def _(half=half):
            down_part(half).start()

    to_matrices(0)
    add_terms(0, ((0, 0, True), (4, 20, True)))
    for half in range(2):
        whole(sg.at[1, pl.ds(18 * half, 18)], sig_sem.at[1, half]).wait()

        @pl.when(has_up)
        def _(half=half):
            up_part(half).start()

    to_matrices(1)
    add_terms(4, ((4, 4, False), (0, 8, False)))

    @pl.when(has_up)
    def _():
        down_copy().wait_recv()

    to_matrices(2)
    add_terms(8, ((4, 12, False),))
    finish(1)
    sigma_flat()

    for c in range(2):
        whole(pk.at[c, pl.ds(0, 31 * 16)], send_sem.at[c]).wait()
        for i in range(4):
            @pl.when(jnp.logical_not(jnp.equal(me, 4 * (2 * i + c) + i)))
            def _(c=c, i=i):
                extra_out(c, i).wait_send()
        whole(ob.at[c, pl.ds(0, 31 * 8)], back_sem.at[c]).wait()

    @pl.when(is_extra)
    def _():
        whole(ob.at[2, pl.ds(0, 31 * 8)], back_sem.at[2]).wait()

    @pl.when(has_up)
    def _():
        u_copy().wait_send()

    @pl.when(has_down)
    def _():
        down_copy().wait_send()

    @pl.when(has_down)
    def _():
        up_copy().wait_recv()

    to_matrices(3)
    add_terms(12, ((0, 16, False),))
    finish(0)

    @pl.when(has_up)
    def _():
        up_copy().wait_send()


def publish_kernel(a, b, a_out, b_out, sems):
    copies = []
    for i, (src, dst) in enumerate(((a, a_out), (b, b_out))):
        for j in range(PIECES):
            part = pl.ds(j * (8 // PIECES), 8 // PIECES)
            copies.append(pltpu.make_async_copy(src.at[part], dst.at[part], sems.at[i, j]))
    for copy in copies:
        copy.start()
    for copy in copies:
        copy.wait()


def flat_view(x):
    return x.reshape(8, 2, 72, 128).transpose(0, 2, 1, 3).reshape(8, 144, 128)


def from_flat(y):
    return y.reshape(8, 72, 2, 128).transpose(0, 2, 1, 3).reshape(2, 4, 2, B * B)


def shards(glesser, wlesser, gret_diag, gret_upper):
    g, w, rd, ru = (flat_view(x) for x in (glesser, wlesser, gret_diag, gret_upper))
    forward, inverse = transforms()
    constants = [jnp.asarray(x) for x in (*two_terms(forward), *two_terms(inverse))]
    vmem = pl.BlockSpec(memory_space=pltpu.VMEM)
    hbm = pl.BlockSpec(memory_space=pl.ANY)
    dma = pltpu.SemaphoreType.DMA
    sigma, new = pl.pallas_call(
        kernel,
        out_shape=[pltpu.VMEM((8, 144, 128), F32)] * 2,
        in_specs=[hbm] * 8,
        out_specs=[vmem] * 2,
        scratch_shapes=[
            pltpu.VMEM((512, 256), BF16),
            pltpu.VMEM((512, 256), BF16),
            pltpu.VMEM((128, 256), BF16),
            pltpu.VMEM((128, 256), BF16),
            pltpu.VMEM((8, 160, 128), F32),
            pltpu.VMEM((8, 160, 128), F32),
            pltpu.VMEM((2, 640, 128), F32),
            pltpu.VMEM((3, PEERS, 16, 128), F32),
            pltpu.VMEM((3, PEERS * 8, 128), F32),
            pltpu.VMEM((2, HALF, 8, 128), F32),
            pltpu.VMEM((HALF, 8, 128), F32),
            pltpu.VMEM((HALF, 8, 128), F32),
            pltpu.VMEM((4, 144, 128), F32),
            pltpu.VMEM((8, 144, 128), F32),
            pltpu.VMEM((8, 144, 128), F32),
            pltpu.VMEM((4 * 384, 128), F32),
            pltpu.VMEM((8, 2, 96, 128), F32),
            pltpu.VMEM((16, 256, 256), BF16),
            pltpu.VMEM((16, 256, 256), BF16),
            pltpu.VMEM((24, 256, 256), BF16),
            pltpu.VMEM((24, 256, 256), BF16),
            pltpu.VMEM((8, 2, 96, 128), F32),
            dma((2, 2)), dma((2,)), dma((4,)), dma((2,)), dma((2, 4)), dma((3,)), dma((3,)), dma((2, 2)), dma((3,)), dma((3,)),
        ],
        compiler_params=pltpu.CompilerParams(collective_id=0, has_side_effects=True, vmem_limit_bytes=VMEM_LIMIT),
        name="update",
    )(g, w, rd, ru, *constants)
    sigma, new = pl.pallas_call(
        publish_kernel,
        out_shape=[jax.ShapeDtypeStruct((8, 144, 128), F32)] * 2,
        in_specs=[vmem] * 2,
        out_specs=[hbm] * 2,
        scratch_shapes=[dma((2, PIECES))],
        name="publish",
    )(*(pltpu.with_memory_space_constraint(x, pltpu.VMEM) for x in (sigma, new)))
    return from_flat(sigma), from_flat(new)


def solution(mesh):
    spec = P("cell", "energy", None, None)
    return jax.shard_map(shards, mesh=mesh, in_specs=(spec,) * 4, out_specs=(spec,) * 2, check_vma=False)
```

```python
import functools

import jax
import jax.numpy as jnp
import ml_dtypes
import numpy as np
from jax import lax
from jax.experimental import pallas as pl
from jax.experimental.pallas import tpu as pltpu
from jax.sharding import PartitionSpec as P

MESH = pl.DeviceIdType.MESH
B = 96
NE = 128
PEERS = 32
HALF = 36
F32 = jnp.float32
BF16 = jnp.bfloat16
PIECES = 4
VMEM_LIMIT = 56 * 1024 * 1024


def two_terms(x):
    high = x.astype(ml_dtypes.bfloat16)
    return high, (x - high.astype(np.float64)).astype(ml_dtypes.bfloat16)


def transforms():
    n = np.arange(NE)
    k = np.arange(NE)
    angle = 2.0 * np.pi / (4 * NE) * ((n[None, :] * (1 - 4 * k[:, None])) % (4 * NE))
    forward = np.zeros((2, 2, NE, NE, 2))
    scale = NE ** -0.5 / NE
    for part in range(2):
        forward[part, 0, :, :, part] = np.cos(angle)
        forward[part, 1, :, :, part] = np.sin(angle)
    inverse = np.concatenate([np.cos(angle).T, np.sin(angle).T], 1) * scale
    return forward.reshape(512, 256), inverse


def split(x):
    high = x.astype(BF16)
    return high, (x - high.astype(F32)).astype(BF16)


def dot3(ah, al, bh, bl, dims=(((1,), (0,)), ((), ()))):
    d = functools.partial(lax.dot_general, dimension_numbers=dims, preferred_element_type=F32)
    return d(ah, bh) + (d(al, bh) + d(ah, bl))


def whole(ref, sem):
    return pltpu.make_async_copy(ref, ref, sem)


def kernel(
    g_hbm, w_hbm, rd_hbm, u_hbm, fh_hbm, fl_hbm, ih_hbm, il_hbm,
    sig_out, new_out,
    fh, fl, ih, il, gv, wv, pk, rv, ob, sg, above, below, ub, rd, ru, km, sf, es_h, es_l, el_h, el_l, total,
    load_sem, ret_sem, mat_sem, send_sem, xsend_sem, recv_sem, back_sem, sig_sem, hop_send, hop_recv,
):
    me = lax.axis_index("energy")
    k = lax.axis_index("cell")
    my_z = me // 4
    my_i = my_z // 2
    my_c = my_z % 2
    is_extra = jnp.equal(me % 4, my_i)
    has_up = k < 7
    has_down = k > 0

    def load_cell(c):
        for j, (source, target) in enumerate(((g_hbm, gv), (w_hbm, wv))):
            pltpu.make_async_copy(source.at[pl.ds(4 * c, 4)], target.at[pl.ds(4 * c, 4), pl.ds(0, 144)], load_sem.at[c, j]).start()

    load_cell(0)

    barrier = pltpu.get_barrier_semaphore()

    def greet(i, carry):
        pl.semaphore_signal(barrier, inc=1, device_id={"energy": lax.rem(me + i, PEERS)}, device_id_type=MESH)
        return carry

    lax.fori_loop(1, PEERS, greet, 0)

    @pl.when(has_up)
    def _():
        pl.semaphore_signal(barrier, inc=1, device_id={"cell": k + 1}, device_id_type=MESH)

    @pl.when(has_down)
    def _():
        pl.semaphore_signal(barrier, inc=1, device_id={"cell": k - 1}, device_id_type=MESH)

    load_cell(1)
    load_rd = pltpu.make_async_copy(rd_hbm, rd, ret_sem.at[0])
    load_ru = pltpu.make_async_copy(u_hbm, ru, ret_sem.at[1])
    load_mats = [
        pltpu.make_async_copy(source, target, mat_sem.at[i])
        for i, (source, target) in enumerate(((fh_hbm, fh), (fl_hbm, fl), (ih_hbm, ih), (il_hbm, il)))
    ]
    for copy in (*load_mats, load_rd, load_ru):
        copy.start()

    row = lax.broadcasted_iota(jnp.int32, (40, 128), 0)
    lane = lax.broadcasted_iota(jnp.int32, (40, 128), 1)
    slot_index = row * 128 + lane
    a_index = (slot_index * 43691) >> 22
    b_index = slot_index - a_index * B
    direct = b_index >= a_index
    diagonal = b_index == a_index
    near = lane >= 48

    def pack(c):
        for which, source in enumerate((gv, wv)):
            pltpu.make_async_copy(
                (g_hbm, w_hbm)[which].at[pl.ds(4 * c, 4)], source.at[pl.ds(4 * c, 4), pl.ds(0, 144)], load_sem.at[c, which]
            ).wait()

            for e in range(4):
                blk = 4 * c + e
                first, far = [], []
                for part in range(2):
                    first.append(source[blk, pl.ds(part, 40, stride=2), :])
                    here = source[blk, pl.ds(72 + part, 40, stride=2), :]
                    after = source[blk, pl.ds(74 + part, 40, stride=2), :]
                    far.append(pltpu.roll(jnp.where(near, here, after), 80, 1))
                re = jnp.where(direct, first[0], far[0])
                re = jnp.where(diagonal, far[1], re)
                im = jnp.where(direct, first[1], far[1])
                base = which * 8 + 2 * e
                pk[c, pl.ds(base, 40, stride=16), :] = re
                pk[c, pl.ds(base + 1, 40, stride=16), :] = im

    def outgoing(c, p):
        return pltpu.make_async_remote_copy(
            src_ref=pk.at[c, pl.ds(p * 16, 16)], dst_ref=rv.at[c, me], send_sem=send_sem.at[c], recv_sem=recv_sem.at[c],
            device_id={"energy": p}, device_id_type=MESH,
        )

    def extra_out(c, i):
        return pltpu.make_async_remote_copy(
            src_ref=pk.at[c, pl.ds((PEERS + i) * 16, 16)], dst_ref=rv.at[2, me], send_sem=xsend_sem.at[c, i],
            recv_sem=recv_sem.at[2], device_id={"energy": 4 * (2 * i + c) + i}, device_id_type=MESH,
        )

    def send(c):
        def start(i, carry):
            p = 4 * lax.rem(me // 4 + 8 + jnp.where(i % 2 == 1, (i % 8 + 1) // 2, -((i % 8) // 2)), 8) + lax.rem(4 - i // 8, 4)

            @pl.when(p != me)
            def _():
                outgoing(c, p).start()

            return carry

        pltpu.make_async_copy(pk.at[c, pl.ds(me * 16, 16)], rv.at[c, me], recv_sem.at[c]).start()
        lax.fori_loop(0, PEERS, start, 0)

        for i in range(4):
            mine = jnp.equal(me, 4 * (2 * i + c) + i)

            @pl.when(jnp.logical_not(mine))
            def _(i=i):
                extra_out(c, i).start()

            @pl.when(mine)
            def _(i=i):
                pltpu.make_async_copy(pk.at[c, pl.ds((PEERS + i) * 16, 16)], rv.at[2, me], recv_sem.at[2]).start()


    pack(0)
    pl.semaphore_wait(barrier, 31 + has_up.astype(jnp.int32) + has_down.astype(jnp.int32))
    send(0)
    pack(1)
    send(1)

    def u_copy():
        return pltpu.make_async_remote_copy(
            src_ref=u_hbm.at[pl.ds(4, 4)], dst_ref=ub, send_sem=hop_send.at[0], recv_sem=hop_recv.at[0],
            device_id={"cell": k + 1}, device_id_type=MESH,
        )

    def down_copy():
        return pltpu.make_async_remote_copy(
            src_ref=sg.at[0], dst_ref=above, send_sem=hop_send.at[1], recv_sem=hop_recv.at[1],
            device_id={"cell": k - 1}, device_id_type=MESH,
        )

    def down_part(half):
        part = pl.ds(18 * half, 18)
        return pltpu.make_async_remote_copy(
            src_ref=sg.at[0, part], dst_ref=above.at[part], send_sem=hop_send.at[1], recv_sem=hop_recv.at[1],
            device_id={"cell": k - 1}, device_id_type=MESH,
        )

    def up_part(half):
        part = pl.ds(18 * half, 18)
        return pltpu.make_async_remote_copy(
            src_ref=sg.at[1, part], dst_ref=below.at[part], send_sem=hop_send.at[2], recv_sem=hop_recv.at[2],
            device_id={"cell": k + 1}, device_id_type=MESH,
        )

    def up_copy():
        return pltpu.make_async_remote_copy(
            src_ref=sg.at[1], dst_ref=below, send_sem=hop_send.at[2], recv_sem=hop_recv.at[2],
            device_id={"cell": k + 1}, device_id_type=MESH,
        )

    @pl.when(has_up)
    def _():
        u_copy().start()

    @pl.when(jnp.logical_not(has_up))
    def _():
        above[...] = jnp.zeros_like(above)

    @pl.when(jnp.logical_not(has_down))
    def _():
        below[...] = jnp.zeros_like(below)
        ub[...] = jnp.zeros_like(ub)

    def place(tile):
        return (tile % 2) * 18 + tile // 2

    def back(slot, c, tile, p):
        return pltpu.make_async_remote_copy(
            src_ref=ob.at[slot, pl.ds(p * 8, 8)], dst_ref=sg.at[c, place(tile)], send_sem=back_sem.at[slot], recv_sem=sig_sem.at[c, tile % 2],
            device_id={"energy": p}, device_id_type=MESH,
        )

    def convolve(slot, c, tile):
        whole(rv.at[slot], recv_sem.at[slot]).wait()
        green = rv[slot, :, 0:8, :].reshape(256, 128)
        screen = rv[slot, :, 8:16, :].reshape(256, 128)
        xh, xl = split(jnp.concatenate([green, screen], 1))
        hat = dot3(fh[...], fl[...], xh, xl)
        xr, xi, yr, yi = (hat[128 * j:128 * j + 128] for j in range(4))
        xrg, xrw, xig, xiw = xr[:, :128], xr[:, 128:], xi[:, :128], xi[:, 128:]
        yrg, yrw, yig, yiw = yr[:, :128], yr[:, 128:], yi[:, :128], yi[:, 128:]
        xx_r = xrg * xrw - xig * xiw
        xx_i = xrg * xiw + xig * xrw
        yy_r = yrg * yrw - yig * yiw
        yy_i = yrg * yiw + yig * yrw
        xy_r = (xrg * yrw - xig * yiw) + (yrg * xrw - yig * xiw)
        xy_i = (xrg * yiw + xig * yrw) + (yrg * xiw + yig * xrw)
        products = jnp.concatenate([jnp.concatenate(z, 0) for z in ((xx_r, xx_i), (yy_r, yy_i), (xy_r, xy_i))], 1)
        zh, zl = split(products)
        out = dot3(ih[...], il[...], zh, zl)
        xx, yy, xy = (out[:, 128 * j:128 * j + 128] for j in range(3))
        position = tile * 128 + lax.broadcasted_iota(jnp.int32, (128, 128), 1)
        on_diagonal = position == ((position * 43241) >> 22) * 97
        ob[slot, pl.ds(0, 128, stride=2), :] = -jnp.where(on_diagonal, xx, xy)
        ob[slot, pl.ds(1, 128, stride=2), :] = jnp.where(on_diagonal, 0.0, xx) - yy

        pltpu.make_async_copy(ob.at[slot, pl.ds(me * 8, 8)], sg.at[c, place(tile)], sig_sem.at[c, tile % 2]).start()

        def start(i, carry):
            back(slot, c, tile, lax.rem(me + PEERS + jnp.where(i % 2 == 1, 16 - i // 2, i // 2 - 16), PEERS)).start()
            return carry

        lax.fori_loop(1, PEERS, start, 0)

    row48 = lax.broadcasted_iota(jnp.int32, (48, 128), 0)
    lane48 = lax.broadcasted_iota(jnp.int32, (48, 128), 1)
    lane8 = lax.broadcasted_iota(jnp.int32, (8, 128), 1)
    lane24 = lax.broadcasted_iota(jnp.int32, (24, 128), 1)
    zero48 = jnp.zeros((80, 128), F32)
    zero32 = jnp.zeros((32, 128), F32)
    inside48 = lane48 < B

    def to_rows(u0, u1, u2, lane):
        r1 = jnp.where(lane < 32, pltpu.roll(u0, 32, 1), pltpu.roll(u1, 32, 1))
        r2 = jnp.where(lane < 64, pltpu.roll(u1, 64, 1), pltpu.roll(u2, 64, 1))
        return u0, r1, r2, pltpu.roll(u2, 96, 1)

    def to_tiles(r0, r1, r2, r3, lane):
        m1, m2, m3 = pltpu.roll(r1, 96, 1), pltpu.roll(r2, 64, 1), pltpu.roll(r3, 32, 1)
        return jnp.where(lane < 96, r0, m1), jnp.where(lane < 64, m1, m2), jnp.where(lane < 32, m2, m3)

    def store_pair(high, low, index, re, im):
        re = jnp.concatenate([re, zero32], 0)
        im = jnp.concatenate([im, zero32], 0)
        rh, rl = split(re)
        mh, ml = split(im)
        for ref, r, m in ((high, rh, mh), (low, rl, ml)):
            ref[index, 0:128, 0:128] = r
            ref[index, 0:128, 128:256] = m
            ref[index, 128:256, 0:128] = -m
            ref[index, 128:256, 128:256] = r

    def flat_store(matrices, out, blk):
        for part in range(2):
            tiles = to_tiles(*(matrices[blk, part, pl.ds(j, 24, stride=4), :] for j in range(4)), lane24)
            for j in range(3):
                out[blk, pl.ds(2 * j + part, 24, stride=6), :] = tiles[j]

    def unpack(index):
        base = 96 * index
        kr = km[base:base + 48, :]
        ki = km[base + 48:base + 96, :]
        krt = -jnp.concatenate([kr, zero48], 0).T
        kit = jnp.concatenate([ki, zero48], 0).T
        less, same = lane48 < row48, lane48 == row48
        top_r = jnp.where(less, krt[:48], jnp.where(same, 0.0, kr))
        top_i = jnp.where(less, kit[:48], ki)
        in_r = jnp.where(less, kr, jnp.where(same, 0.0, krt[:48]))
        in_i = jnp.where(less, ki, jnp.where(same, kr, kit[:48]))
        low_r = jnp.where(lane48 < 48, krt[48:96], pltpu.roll(in_r, 48, 1))
        low_i = jnp.where(lane48 < 48, kit[48:96], pltpu.roll(in_i, 48, 1))
        re = jnp.concatenate([jnp.where(inside48, top_r, 0.0), jnp.where(inside48, low_r, 0.0)], 0)
        im = jnp.concatenate([jnp.where(inside48, top_i, 0.0), jnp.where(inside48, low_i, 0.0)], 0)
        store_pair(es_h, es_l, index, re, im)
        if index < 8:
            sf[index, 0] = re
            sf[index, 1] = im

    def to_matrices(array):
        def take(t):
            t = place(t)
            return sg[array, t] if array < 2 else (above[t] if array == 2 else below[t])

        for q in range(12):
            for j, r in enumerate(to_rows(take(3 * q), take(3 * q + 1), take(3 * q + 2), lane8)):
                km[pl.ds(array * 384 + 4 * q + j, 8, stride=48), :] = r
        for index in range(4 * array, 4 * array + 4):
            unpack(index)

    lane96 = lax.broadcasted_iota(jnp.int32, (96, 128), 1)

    def matrix(source, blk, part):
        u = [source[blk, pl.ds(2 * j + part, 24, stride=6), :] for j in range(3)]
        for j, r in enumerate(to_rows(*u, lane24)):
            sf[blk, part, pl.ds(j, 24, stride=4), :] = r
        return jnp.where(lane96 < B, sf[blk, part], 0.0)

    def flip(x):
        return jnp.concatenate([x, zero32], 0).T[:96]

    def diag_prep(blk, carry):
        store_pair(el_h, el_l, blk, matrix(rd, blk, 0), matrix(rd, blk, 1))
        return carry

    def upper_prep(blk, carry):
        re, im = matrix(ru, blk, 0), matrix(ru, blk, 1)
        store_pair(el_h, el_l, 8 + blk, re, im)

        @pl.when(blk < 4)
        def _():
            store_pair(el_h, el_l, 20 + blk, flip(re), flip(im))

        return carry

    def below_prep(blk, carry):
        store_pair(el_h, el_l, 16 + blk, flip(matrix(ub, blk, 0)), flip(matrix(ub, blk, 1)))
        return carry

    transposed = (((1,), (1,)), ((), ()))

    def add_terms(middle, pairs):
        for e in range(4):
            left_h = jnp.concatenate([el_h[left + e, 0:96, :] for _, left, _ in pairs], 0)
            left_l = jnp.concatenate([el_l[left + e, 0:96, :] for _, left, _ in pairs], 0)
            xh, xl = split(dot3(left_h, left_l, es_h[middle + e], es_l[middle + e]))
            for i, (blk, left, first) in enumerate(pairs):
                rows = slice(96 * i, 96 * i + 96)
                value = dot3(xh[rows], xl[rows], el_h[left + e], el_l[left + e], transposed)
                for part in range(2):
                    half = value[:, 128 * part:128 * part + 128]
                    if first:
                        total[blk + e, part] = half
                    else:
                        total[blk + e, part] += half

    def finish(c):
        for blk in range(4 * c, 4 * c + 4):
            flat_store(total, new_out, blk)

    def sigma_flat():
        for blk in range(8):
            flat_store(sf, sig_out, blk)

    def convolve_cell(c):
        def step(j, inner):
            slot = jnp.where(j == 0, c, 2)
            tile = jnp.where(j == 0, me, PEERS + my_i)
            convolve(slot, c, tile)
            return inner

        lax.fori_loop(0, 1 + jnp.where(jnp.logical_and(is_extra, my_c == c), 1, 0), step, 0)

    load_rd.wait()
    lax.fori_loop(0, 8, diag_prep, 0)
    for copy in load_mats:
        copy.wait()
    convolve_cell(0)
    load_ru.wait()
    lax.fori_loop(0, 8, upper_prep, 0)
    convolve_cell(1)

    @pl.when(has_down)
    def _():
        u_copy().wait_recv()

    lax.fori_loop(0, 4, below_prep, 0)

    for half in range(2):
        whole(sg.at[0, pl.ds(18 * half, 18)], sig_sem.at[0, half]).wait()

        @pl.when(has_down)
        def _(half=half):
            down_part(half).start()

    to_matrices(0)
    for half in range(2):
        whole(sg.at[1, pl.ds(18 * half, 18)], sig_sem.at[1, half]).wait()

        @pl.when(has_up)
        def _(half=half):
            up_part(half).start()

    add_terms(0, ((0, 0, True), (4, 20, True)))
    to_matrices(1)
    add_terms(4, ((4, 4, False), (0, 8, False)))

    @pl.when(has_up)
    def _():
        down_copy().wait_recv()

    to_matrices(2)
    add_terms(8, ((4, 12, False),))
    finish(1)
    sigma_flat()

    for c in range(2):
        whole(pk.at[c, pl.ds(0, 31 * 16)], send_sem.at[c]).wait()
        for i in range(4):
            @pl.when(jnp.logical_not(jnp.equal(me, 4 * (2 * i + c) + i)))
            def _(c=c, i=i):
                extra_out(c, i).wait_send()
        whole(ob.at[c, pl.ds(0, 31 * 8)], back_sem.at[c]).wait()

    @pl.when(is_extra)
    def _():
        whole(ob.at[2, pl.ds(0, 31 * 8)], back_sem.at[2]).wait()

    @pl.when(has_up)
    def _():
        u_copy().wait_send()

    @pl.when(has_down)
    def _():
        down_copy().wait_send()

    @pl.when(has_down)
    def _():
        up_copy().wait_recv()

    to_matrices(3)
    add_terms(12, ((0, 16, False),))
    finish(0)

    @pl.when(has_up)
    def _():
        up_copy().wait_send()


def publish_kernel(a, b, a_out, b_out, sems):
    copies = []
    for i, (src, dst) in enumerate(((a, a_out), (b, b_out))):
        for j in range(PIECES):
            part = pl.ds(j * (8 // PIECES), 8 // PIECES)
            copies.append(pltpu.make_async_copy(src.at[part], dst.at[part], sems.at[i, j]))
    for copy in copies:
        copy.start()
    for copy in copies:
        copy.wait()


def flat_view(x):
    return x.reshape(8, 2, 72, 128).transpose(0, 2, 1, 3).reshape(8, 144, 128)


def from_flat(y):
    return y.reshape(8, 72, 2, 128).transpose(0, 2, 1, 3).reshape(2, 4, 2, B * B)


def shards(glesser, wlesser, gret_diag, gret_upper):
    g, w, rd, ru = (flat_view(x) for x in (glesser, wlesser, gret_diag, gret_upper))
    forward, inverse = transforms()
    constants = [jnp.asarray(x) for x in (*two_terms(forward), *two_terms(inverse))]
    vmem = pl.BlockSpec(memory_space=pltpu.VMEM)
    hbm = pl.BlockSpec(memory_space=pl.ANY)
    dma = pltpu.SemaphoreType.DMA
    sigma, new = pl.pallas_call(
        kernel,
        out_shape=[pltpu.VMEM((8, 144, 128), F32)] * 2,
        in_specs=[hbm] * 8,
        out_specs=[vmem] * 2,
        scratch_shapes=[
            pltpu.VMEM((512, 256), BF16),
            pltpu.VMEM((512, 256), BF16),
            pltpu.VMEM((128, 256), BF16),
            pltpu.VMEM((128, 256), BF16),
            pltpu.VMEM((8, 160, 128), F32),
            pltpu.VMEM((8, 160, 128), F32),
            pltpu.VMEM((2, 640, 128), F32),
            pltpu.VMEM((3, PEERS, 16, 128), F32),
            pltpu.VMEM((3, PEERS * 8, 128), F32),
            pltpu.VMEM((2, HALF, 8, 128), F32),
            pltpu.VMEM((HALF, 8, 128), F32),
            pltpu.VMEM((HALF, 8, 128), F32),
            pltpu.VMEM((4, 144, 128), F32),
            pltpu.VMEM((8, 144, 128), F32),
            pltpu.VMEM((8, 144, 128), F32),
            pltpu.VMEM((4 * 384, 128), F32),
            pltpu.VMEM((8, 2, 96, 128), F32),
            pltpu.VMEM((16, 256, 256), BF16),
            pltpu.VMEM((16, 256, 256), BF16),
            pltpu.VMEM((24, 256, 256), BF16),
            pltpu.VMEM((24, 256, 256), BF16),
            pltpu.VMEM((8, 2, 96, 128), F32),
            dma((2, 2)), dma((2,)), dma((4,)), dma((2,)), dma((2, 4)), dma((3,)), dma((3,)), dma((2, 2)), dma((3,)), dma((3,)),
        ],
        compiler_params=pltpu.CompilerParams(collective_id=0, has_side_effects=True, vmem_limit_bytes=VMEM_LIMIT),
        name="update",
    )(g, w, rd, ru, *constants)
    sigma, new = pl.pallas_call(
        publish_kernel,
        out_shape=[jax.ShapeDtypeStruct((8, 144, 128), F32)] * 2,
        in_specs=[vmem] * 2,
        out_specs=[hbm] * 2,
        scratch_shapes=[dma((2, PIECES))],
        name="publish",
    )(*(pltpu.with_memory_space_constraint(x, pltpu.VMEM) for x in (sigma, new)))
    return from_flat(sigma), from_flat(new)


def solution(mesh):
    spec = P("cell", "energy", None, None)
    return jax.shard_map(shards, mesh=mesh, in_specs=(spec,) * 4, out_specs=(spec,) * 2, check_vma=False)
```
